512 devices in a mesh: gx: 32 (over x_lo, z, core), gy: 16 (over x_hi, y).
Axes of the slice: x: 4 (x_hi: 2, x_lo: 2; x = x_hi * 2 + x_lo), y: 8, z: 8, core: 2. Of those that a mesh axis runs over, the one named last changes fastest.
Arguments:
- noise: float32 [512, 1024, 512], P('gx', 'gy'), may hold values from -6 to 6
- rate: float32 [512, 1024], P('gx', 'gy'), may hold values from -0.3 to 0.3
- coupling: float32 [512, 1024], P('gx', 'gy'), may hold values from 0.05 to 0.2
- vertical: float32 [64, 64], replicated, may hold values from -0.12 to 0.12
- coeffs: float32 [4], replicated, may hold values from 0.3 to 1
- columns: int32 [512, 64], P(('gx', 'gy')), may hold values from 0 to 1023
- slots: int32 [512, 64], P(('gx', 'gy')), may hold values from 0 to 63, each once within a row
Outputs:
- sample: float32 [512, 1024, 512], P('gx', 'gy')
- grad_blocks: float32 [32768, 1024], P(('gx', 'gy'))
The draws below stay inside these ranges and needn't reach their ends.
Inputs may be any that keep to these rules, and one draw needn't show every extreme that they name: Each row of slots is a permutation; slot k is owned by the device at gx index k // 2 in the same gy column.
All inputs are finite; a program needn't handle non-finite values.
Results may differ from the reference program's by a relative error of at most 0.0002.
Values sent between devices are 32-bit elements; how exact they have to be, the bound alone decides.
A program may use at most 64 MiB of HBM per device.

```python
import jax
import jax.numpy as jnp
from jax import lax

DEPTH = 64
DRAWS = 8
STEPS = 3
CX = 16
CY = 64
PER_PEER = 2
SENS_DEV = 64
NX = 512
NY = 1024
N_GX = 32
N_GY = 16


def with_ends(entries, stream_key, smallest, high):
    spot = [jax.random.randint(jax.random.fold_in(stream_key, axis), (), 0, length) for axis, length in enumerate(entries.shape)]
    longest = entries.shape.index(max(entries.shape))
    next_to = spot[:longest] + [(spot[longest] + 1) % entries.shape[longest]] + spot[longest + 1:]
    return entries.at[tuple(spot)].set(smallest).at[tuple(next_to)].set(high)


def levels(rng, shape, split, smallest, high):
    def one(dim, shards_of):
        draws = jax.random.uniform(jax.random.fold_in(jax.random.fold_in(rng, 6), dim), (shards_of,), jnp.float32, smallest / len(split), high / len(split))
        return jnp.repeat(jnp.exp(draws), shape[dim] // shards_of).reshape((-1,) + (1,) * (len(shape) - dim - 1))

    factor_of = one(*split[0])
    for cut in split[1:]:
        factor_of = factor_of * one(*cut)
    return factor_of


def gaussian(key, shape, scale, reach, pieces=(), held_as=jnp.bfloat16):
    values = jax.random.normal(key, shape, jnp.float32) * scale
    if len(pieces) > 0:
        values = levels(key, shape, pieces, -0.22, 0.18) * values
    return jnp.clip(values, min=-reach, max=reach).astype(held_as)


def setup_inputs(seed: int = 0) -> dict:
    key_list = jax.random.split(jax.random.key(seed), 8)
    return {
        "noise": gaussian(key_list[0], (NX, NY, DRAWS * DEPTH), 1.0, 6.0, ((0, 32), (1, 16)), jnp.float32),
        "rate": jnp.clip(jax.random.uniform(key_list[1], (NX, NY), jnp.float32, -0.3, 0.3) * levels(key_list[1], (NX, NY), ((0, 32), (1, 16)), -0.4, 0.0), -0.3, 0.3),
        "coupling": jnp.clip(0.05 + 0.15 * jax.random.uniform(key_list[2], (NX, NY), jnp.float32) ** levels(key_list[2], (NX, NY), ((0, 32), (1, 16)), -0.2, 0.2), 0.05, 0.2),
        "vertical": gaussian(key_list[3], (DEPTH, DEPTH), 0.02, 0.12, (), jnp.float32),
        "coeffs": jnp.clip(jax.random.uniform(key_list[4], (STEPS + 1,), jnp.float32, 0.3, 1.0), 0.3, 1.0),
        "columns": with_ends(jax.random.randint(key_list[5], (N_GX * N_GY, SENS_DEV), 0, CX * CY), jax.random.fold_in(key_list[5], 1), 0, (CX * CY) - 1).astype(jnp.int32),
        "slots": jax.vmap(lambda own: jax.random.permutation(own, SENS_DEV))(jax.random.split(key_list[6], (N_GX * N_GY))).reshape((N_GX * N_GY, SENS_DEV)).astype(jnp.int32),
    }


def operate(field, rate, coupling, vertical):
    padded = jnp.pad(field, ((1, 1), (1, 1), (0, 0)))
    beside = padded[2:, 1:-1] + padded[:-2, 1:-1] + padded[1:-1, 2:] + padded[1:-1, :-2]
    column = jnp.dot(field.reshape(-1, DEPTH), vertical.T, precision=lax.Precision.HIGHEST, preferred_element_type=jnp.float32).reshape(field.shape)
    return rate[:, :, None] * field + column - coupling[:, :, None] * beside


def reference(noise, rate, coupling, vertical, coeffs, columns, slots):
    fields = noise.reshape(NX, NY, DRAWS, DEPTH).transpose(2, 0, 1, 3)

    def series(start):
        first = operate(start, rate, coupling, vertical)
        second = 2.0 * operate(first, rate, coupling, vertical) - start
        third = 2.0 * operate(second, rate, coupling, vertical) - first
        return coeffs[0] * start + coeffs[1] * first + coeffs[2] * second + coeffs[3] * third

    sample = lax.map(series, fields).transpose(1, 2, 0, 3).reshape(NX, NY, DRAWS * DEPTH)
    flat_field = sample.reshape(NX * NY, DRAWS * DEPTH)
    device_row = jnp.arange(N_GX * N_GY, dtype=jnp.int32)[:, None]
    row_x = (device_row // N_GY) * CX + columns // CY
    row_y = (device_row % N_GY) * CY + columns % CY

    def pick(cell_x, cell_y):
        valid = (cell_x >= 0) & (cell_x < NX) & (cell_y >= 0) & (cell_y < NY)
        where_at = jnp.clip(cell_x, 0, NX - 1) * NY + jnp.clip(cell_y, 0, NY - 1)
        return jnp.where(valid[..., None], flat_field[where_at], jnp.float32(0.0))

    center = pick(row_x, row_y)
    slope_x = (pick(row_x + 1, row_y) - pick(row_x - 1, row_y)) * 0.5
    slope_y = (pick(row_x, row_y + 1) - pick(row_x, row_y - 1)) * 0.5
    lead = center.shape[:2]
    grouped = center.reshape(lead + (DRAWS, DEPTH))
    centred = (grouped - jnp.mean(grouped, axis=2, keepdims=True)).reshape(lead + (DRAWS * DEPTH,))
    block = jnp.concatenate([centred * slope_x, centred * slope_y], axis=-1)
    ordered = jax.vmap(lambda rows, place: jnp.zeros_like(rows).at[place].set(rows))(block, slots)
    ordered = ordered.reshape(N_GX, N_GY, N_GX, PER_PEER, 2 * DRAWS * DEPTH).transpose(2, 1, 0, 3, 4)
    return sample, ordered.reshape(N_GX * N_GY * SENS_DEV, 2 * DRAWS * DEPTH)
```

```python
import functools

import jax
import jax.numpy as jnp
from jax import lax
from jax.experimental import pallas as pl
from jax.experimental.pallas import tpu as pltpu
from jax.sharding import PartitionSpec as P

MESH = pl.DeviceIdType.MESH
HIGHEST = lax.Precision.HIGHEST
F32 = jnp.float32
BF16 = jnp.bfloat16
LANES = 128
PAD = 8


def split2(value):
    high = value.astype(BF16)
    return high, (value - high.astype(F32)).astype(BF16)


def iota(shape, dim):
    return lax.broadcasted_iota(jnp.int32, shape, dim)


def dot_t(a, b):
    return lax.dot_general(a, b, (((1,), (1,)), ((), ())), precision=HIGHEST, preferred_element_type=F32)


def dot(a, b):
    return jnp.dot(a, b, precision=HIGHEST, preferred_element_type=F32)


def kernel(n_gx, n_gy, noise, rate, coupling, vertical, slots, columns, coeffs, sample, grads,
           e0, e1, e2, e3, rate_b, coup_b, weights, y_out, y_in, g_c, g_x, g_y, ready,
           load_sem, xs_sem, xr_sem, ys_sem, yr_sem, as_sem, ar_sem, store_sem, own_sem):
    cx, cy, width = noise.shape
    depth = vertical.shape[0]
    sensors = slots.shape[1]
    reps = width // LANES
    me = lax.axis_index("gx")
    my = lax.axis_index("gy")
    fields = (e0, e1, e2, e3)
    own = pl.ds(PAD, cy)

    barrier = pltpu.get_barrier_semaphore()

    def greet(k, carry):
        pl.semaphore_signal(barrier, inc=1, device_id=(lax.rem(me + k, n_gx), my), device_id_type=MESH)
        return carry

    lax.fori_loop(1, n_gx, greet, 0)

    @pl.when(my > 0)
    def _():
        pl.semaphore_signal(barrier, inc=1, device_id=(me, my - 1), device_id_type=MESH)

    @pl.when(my < n_gy - 1)
    def _():
        pl.semaphore_signal(barrier, inc=1, device_id=(me, my + 1), device_id_type=MESH)

    load = pltpu.make_async_copy(noise, e0.at[pl.ds(1, cx), own, :], load_sem)
    load.start()

    zero_row = jnp.zeros((cy, width), F32)
    zero_col = jnp.zeros((cx, width), F32)

    @pl.when(me == 0)
    def _():
        for field in fields:
            field[0, own, :] = zero_row

    @pl.when(me == n_gx - 1)
    def _():
        for field in fields:
            field[cx + 1, own, :] = zero_row

    @pl.when(my == 0)
    def _():
        for r in range(4):
            y_in[r, 0] = zero_col

    @pl.when(my == n_gy - 1)
    def _():
        for r in range(4):
            y_in[r, 1] = zero_col

    diag = iota((cy, cy), 0) == iota((cy, cy), 1)

    def spread(i, carry):
        for src, dst in ((rate, rate_b), (coupling, coup_b)):
            row = jnp.broadcast_to(src[pl.ds(i, 1), :], (cy, cy))
            col = jnp.sum(jnp.where(diag, row, 0.0), axis=1, keepdims=True)
            dst[i] = jnp.broadcast_to(col, (cy, LANES))
        return carry

    lax.fori_loop(0, cx, spread, 0)

    pl.semaphore_wait(barrier, n_gx - 1 + jnp.where(my > 0, 1, 0) + jnp.where(my < n_gy - 1, 1, 0))

    def x_copy(r, side):
        src_row = 1 if side == 0 else cx
        src = fields[r].at[src_row, own, :]
        if r == 0:
            src = noise.at[src_row - 1]
        return pltpu.make_async_remote_copy(
            src_ref=src, dst_ref=fields[r].at[cx + 1 if side == 0 else 0, own, :],
            send_sem=xs_sem.at[r, side], recv_sem=xr_sem.at[r, side],
            device_id=(me - 1 if side == 0 else me + 1, my), device_id_type=MESH)

    def y_copy(r, side):
        return pltpu.make_async_remote_copy(
            src_ref=y_out.at[r, side], dst_ref=y_in.at[r, 1 - side],
            send_sem=ys_sem.at[r, side], recv_sem=yr_sem.at[r, side],
            device_id=(me, my - 1 if side == 0 else my + 1), device_id_type=MESH)

    x_has = (me > 0, me < n_gx - 1)
    y_has = (my > 0, my < n_gy - 1)

    def send_x(r):
        for side in range(2):
            @pl.when(x_has[side])
            def _():
                x_copy(r, side).start()

    def send_y(r):
        field = fields[r]
        for i in range(cx):
            y_out[r, 0, i:i + 1, :] = field[i + 1, PAD:PAD + 1, :]
            y_out[r, 1, i:i + 1, :] = field[i + 1, PAD + cy - 1:PAD + cy, :]
        for side in range(2):
            @pl.when(y_has[side])
            def _():
                y_copy(r, side).start()

    def receive(r):
        field = fields[r]
        for side in range(2):
            @pl.when(y_has[1 - side])
            def _():
                y_copy(r, side).wait_recv()
        for i in range(cx):
            field[i + 1, PAD - 1:PAD, :] = y_in[r, 0, i:i + 1, :]
            field[i + 1, PAD + cy:PAD + cy + 1, :] = y_in[r, 1, i:i + 1, :]
        for side in range(2):
            @pl.when(x_has[1 - side])
            def _():
                x_copy(r, side).wait_recv()

    def sent(r):
        for side in range(2):
            @pl.when(x_has[side])
            def _():
                x_copy(r, side).wait_send()

            @pl.when(y_has[side])
            def _():
                y_copy(r, side).wait_send()

    q0 = coeffs[0] - coeffs[2]
    q1 = coeffs[1] - 3.0 * coeffs[3]
    q2 = 2.0 * coeffs[2]
    q3 = 4.0 * coeffs[3]

    def lateral(r, i, low, high):
        old, new = fields[r], fields[r + 1]
        rows = pl.ds(PAD + low, high - low)
        beside = (old[i, rows, :] + old[i + 2, rows, :]) + (
            old[i + 1, PAD - 1 + low:PAD - 1 + high, :] + old[i + 1, PAD + 1 + low:PAD + 1 + high, :])
        a = rate_b[i, low:high, :]
        b = coup_b[i, low:high, :]
        if r == 0:
            a, b = q3 * a, q3 * b
        a = jnp.concatenate([a] * reps, axis=1)
        b = jnp.concatenate([b] * reps, axis=1)
        new[i + 1, rows, :] = new[i + 1, rows, :] + a * old[i + 1, rows, :] - b * beside

    def inner(r):
        def row(i, carry):
            lateral(r, i, 8, cy - 8)
            return carry

        lax.fori_loop(1, cx - 1, row, 0)

    def outer(r):
        lateral(r, 0, 0, cy)
        lateral(r, cx - 1, 0, cy)

        def row(i, carry):
            lateral(r, i, 0, 8)
            lateral(r, i, cy - 8, cy)
            return carry

        lax.fori_loop(1, cx - 1, row, 0)

    send_x(0)
    load.wait()
    send_y(0)

    block = 2 * LANES
    pick = (iota((block, depth), 0) % depth == iota((block, depth), 1)).astype(F32)
    tiled = dot_t(dot_t(pick, vertical[...]), pick)
    same = iota((block, block), 0) // depth == iota((block, block), 1) // depth
    eye = jnp.where(iota((block, block), 0) == iota((block, block), 1), 1.0, 0.0)
    v1 = jnp.where(same, tiled, 0.0)
    v2 = dot(v1, v1)
    v3 = dot(v1, v2)
    polys = (
        q2 * eye + (3.0 * q3) * v1,
        q1 * eye + (2.0 * q2) * v1 + (3.0 * q3) * v2,
        q0 * eye + q1 * v1 + q2 * v2 + q3 * v3,
    )
    for k, poly in enumerate(polys):
        high, low = split2(poly)
        weights[k, 0:block, :] = high
        weights[k, block:2 * block, :] = high
        weights[k, 2 * block:3 * block, :] = low

    group = 4

    def columns_of(k):
        def part(g, carry):
            rows = pl.ds(1 + g * group, group)
            for half in range(width // block):
                lanes = slice(half * block, (half + 1) * block)
                high, low = split2(e0[rows, own, lanes].reshape(group * cy, block))
                out = jnp.dot(jnp.concatenate([high, low, high], axis=1), weights[k],
                              preferred_element_type=F32)
                fields[k + 1][rows, own, lanes] = out.reshape(group, cy, block)
            return carry

        lax.fori_loop(0, cx // group, part, 0)

    columns_of(0)
    inner(0)
    receive(0)
    outer(0)
    send_x(1)
    send_y(1)
    columns_of(1)
    inner(1)
    receive(1)
    outer(1)
    send_x(2)
    send_y(2)
    columns_of(2)
    inner(2)
    receive(2)
    outer(2)
    send_x(3)
    send_y(3)
    store = pltpu.make_async_copy(e3.at[pl.ds(1, cx), own, :], sample, store_sem)
    store.start()
    receive(3)

    def gather(k, carry):
        place = columns[0, k]
        i = place // cy
        j = place % cy + PAD
        spot = pl.ds(k, 1)
        g_c[spot, :] = e3[i + 1, pl.ds(j, 1), :]
        g_x[spot, :] = (e3[i + 2, pl.ds(j, 1), :] - e3[i, pl.ds(j, 1), :]) * 0.5
        g_y[spot, :] = (e3[i + 1, pl.ds(j + 1, 1), :] - e3[i + 1, pl.ds(j - 1, 1), :]) * 0.5
        return carry

    lax.fori_loop(0, sensors, gather, 0, unroll=4)

    draws = width // depth
    center = g_c[...]
    total = center[:, 0:LANES]
    for t in range(1, reps):
        total = total + center[:, t * LANES:(t + 1) * LANES]
    total = (total + pltpu.roll(total, depth, axis=1)) * (1.0 / draws)
    to_slot = (iota((sensors, sensors), 0) == slots[...]).astype(BF16)
    for d, slope in enumerate((g_x, g_y)):
        for t in range(reps):
            lanes = slice(t * LANES, (t + 1) * LANES)
            value = (center[:, lanes] - total) * slope[:, lanes]
            first = value.astype(BF16)
            rest = value - first.astype(F32)
            second, third = split2(rest)
            out = (jnp.dot(to_slot, first, preferred_element_type=F32)
                   + jnp.dot(to_slot, second, preferred_element_type=F32)
                   + jnp.dot(to_slot, third, preferred_element_type=F32))
            ready[pl.ds(d * reps + t, sensors, stride=2 * reps), :] = out

    per = ready.shape[0] // n_gx
    spot = pl.ds(pl.multiple_of(me * per, per), per)

    def to_peer(k):
        peer = lax.rem(me + k, n_gx)
        return pltpu.make_async_remote_copy(
            src_ref=ready.at[pl.ds(pl.multiple_of(peer * per, per), per), :], dst_ref=grads.at[spot, :],
            send_sem=as_sem.at[k], recv_sem=ar_sem.at[k], device_id=(peer, my), device_id_type=MESH)

    def start(k, carry):
        to_peer(k).start()
        return carry

    lax.fori_loop(1, n_gx, start, 0)
    keep = pltpu.make_async_copy(ready.at[spot, :], grads.at[spot, :], own_sem)
    keep.start()
    for r in range(4):
        sent(r)
    store.wait()
    keep.wait()

    def finish(k, carry):
        copy = to_peer(k)
        copy.wait_send()
        copy.wait_recv()
        return carry

    lax.fori_loop(1, n_gx, finish, 0)


def shards(n_gx, n_gy, noise, rate, coupling, vertical, coeffs, columns, slots):
    cx, cy, width = noise.shape
    sensors = slots.shape[1]
    parts = 2 * width // LANES
    vmem = pl.BlockSpec(memory_space=pltpu.VMEM)
    smem = pl.BlockSpec(memory_space=pltpu.SMEM)
    hbm = pl.BlockSpec(memory_space=pl.ANY)
    field = pltpu.VMEM((cx + 2, cy + 2 * PAD, width), F32)
    dma = pltpu.SemaphoreType.DMA
    sample, grads = pl.pallas_call(
        functools.partial(kernel, n_gx, n_gy),
        out_shape=(jax.ShapeDtypeStruct(noise.shape, F32),
                   jax.ShapeDtypeStruct((sensors * parts, LANES), F32)),
        in_specs=[hbm, vmem, vmem, vmem, vmem, smem, smem],
        out_specs=(hbm, hbm),
        scratch_shapes=[
            field, field, field, field,
            pltpu.VMEM((cx, cy, LANES), F32), pltpu.VMEM((cx, cy, LANES), F32),
            pltpu.VMEM((3, 6 * LANES, 2 * LANES), BF16),
            pltpu.VMEM((4, 2, cx, width), F32), pltpu.VMEM((4, 2, cx, width), F32),
            pltpu.VMEM((sensors, width), F32), pltpu.VMEM((sensors, width), F32), pltpu.VMEM((sensors, width), F32),
            pltpu.VMEM((sensors * parts, LANES), F32),
            dma, dma((4, 2)), dma((4, 2)), dma((4, 2)), dma((4, 2)),
            dma((n_gx,)), dma((n_gx,)), dma, dma,
        ],
        compiler_params=pltpu.CompilerParams(
            collective_id=0, has_side_effects=True, vmem_limit_bytes=40 << 20),
    )(noise, rate, coupling, vertical, slots, columns, coeffs)
    return sample, grads.reshape(sensors, parts * LANES)


def solution(mesh):
    placed = (
        P("gx", "gy", None),
        P("gx", "gy"),
        P("gx", "gy"),
        P(),
        P(),
        P(("gx", "gy"), None),
        P(("gx", "gy"), None),
    )
    return jax.shard_map(
        functools.partial(shards, mesh.shape["gx"], mesh.shape["gy"]),
        mesh=mesh,
        in_specs=placed,
        out_specs=(P("gx", "gy", None), P(("gx", "gy"), None)),
        check_vma=False,
    )
```

```python
import functools

import jax
import jax.numpy as jnp
from jax import lax
from jax.experimental import pallas as pl
from jax.experimental.pallas import tpu as pltpu
from jax.sharding import PartitionSpec as P

MESH = pl.DeviceIdType.MESH
HIGHEST = lax.Precision.HIGHEST
F32 = jnp.float32
BF16 = jnp.bfloat16
LANES = 128
GROUP = 4
PAD = 16


def split2(value):
    high = value.astype(BF16)
    return high, (value - high.astype(F32)).astype(BF16)


def iota(shape, dim):
    return lax.broadcasted_iota(jnp.int32, shape, dim)


def dot_t(a, b):
    return lax.dot_general(a, b, (((1,), (1,)), ((), ())), precision=HIGHEST, preferred_element_type=F32)


def dot(a, b):
    return jnp.dot(a, b, precision=HIGHEST, preferred_element_type=F32)


def kernel(n_gx, n_gy, noise, rate_in, coupling_in, vertical_in, slots_in, columns_in, coeffs_in, sample, grads,
           rate, coupling, vertical, slots, columns, coeffs, e0, e1, e2, e3, total, rate_b, coup_b, weights,
           y_out, y_in, beside_coef, spots_v, spots, g_c, ready,
           small_sem, load_sem, xs_sem, xr_sem, ys_sem, yr_sem, cs_sem, cr_sem, ks_sem, kr_sem, as_sem, ar_sem, store_sem, own_sem, spot_sem):
    cx, cy, width = noise.shape
    depth = vertical.shape[0]
    sensors = slots.shape[1]
    reps = width // LANES
    me = lax.axis_index("gx")
    my = lax.axis_index("gy")
    fields = (e0, e1, e2, e3)
    own = pl.ds(PAD, cy)
    x_has = (me > 0, me < n_gx - 1)
    y_has = (my > 0, my < n_gy - 1)
    both_sides = [(sx, sy) for sx in range(2) for sy in range(2)]

    def x_at(side):
        return me - 1 if side == 0 else me + 1

    def y_at(side):
        return my - 1 if side == 0 else my + 1

    barrier = pltpu.get_barrier_semaphore()

    def greet(k, carry):
        pl.semaphore_signal(barrier, inc=1, device_id=(lax.rem(me + k, n_gx), my), device_id_type=MESH)
        return carry

    lax.fori_loop(1, n_gx, greet, 0)
    beside_y = [(y_has[sy], (me, y_at(sy))) for sy in range(2)]
    beside_y += [(jnp.logical_and(x_has[sx], y_has[sy]), (x_at(sx), y_at(sy))) for sx, sy in both_sides]
    arrivals = n_gx - 1
    for there, device in beside_y:
        arrivals = arrivals + jnp.where(there, 1, 0)

        @pl.when(there)
        def _():
            pl.semaphore_signal(barrier, inc=1, device_id=device, device_id_type=MESH)

    load = pltpu.make_async_copy(noise, e0.at[pl.ds(2, cx), own, :], load_sem)
    load.start()
    small = [
        pltpu.make_async_copy(src, dst, small_sem.at[i])
        for i, (src, dst) in enumerate((
            (rate_in, rate), (coupling_in, coupling), (vertical_in, vertical),
            (slots_in, slots), (columns_in, columns), (coeffs_in, coeffs)))
    ]
    for copy in small:
        copy.start()

    for side in range(2):
        @pl.when(jnp.logical_not(x_has[side]))
        def _():
            for field in (e0, e2):
                for i in (0, 1) if side == 0 else (cx + 2, cx + 3):
                    field[i] = jnp.zeros(field.shape[1:], F32)
            beside_coef[1 - side] = jnp.zeros(beside_coef.shape[1:], F32)

        @pl.when(jnp.logical_not(y_has[side]))
        def _():
            for field in (e0, e2):
                for i in (1, cx + 2):
                    block = pl.ds(PAD - 8 if side == 0 else PAD + cy, 8)
                    field[i, block, :] = jnp.zeros((8, width), F32)
            for r in range(2):
                y_in[r, side] = jnp.zeros(y_in.shape[2:], F32)
            beside_coef[3 - side] = jnp.zeros(beside_coef.shape[1:], F32)

    pl.semaphore_wait(barrier, arrivals)

    def x_copy(r, side):
        field = fields[2 * r]
        row = 0 if side == 0 else cx - 2
        src = noise.at[pl.ds(row, 2)] if r == 0 else field.at[pl.ds(row + 2, 2), own, :]
        return pltpu.make_async_remote_copy(
            src_ref=src, dst_ref=field.at[pl.ds(cx + 2 if side == 0 else 0, 2), own, :],
            send_sem=xs_sem.at[r, side], recv_sem=xr_sem.at[r, side],
            device_id=(x_at(side), my), device_id_type=MESH)

    def y_copy(r, side):
        return pltpu.make_async_remote_copy(
            src_ref=y_out.at[r, side], dst_ref=y_in.at[r, 1 - side],
            send_sem=ys_sem.at[r, side], recv_sem=yr_sem.at[r, side],
            device_id=(me, y_at(side)), device_id_type=MESH)

    def corner_copy(r, sx, sy):
        field = fields[2 * r]
        row = 0 if sx == 0 else cx - 1
        col = 0 if sy == 0 else cy - 8
        src = noise.at[row, pl.ds(col, 8), :] if r == 0 else field.at[row + 2, pl.ds(PAD + col, 8), :]
        return pltpu.make_async_remote_copy(
            src_ref=src, dst_ref=field.at[cx + 2 if sx == 0 else 1, pl.ds(PAD + cy if sy == 0 else PAD - 8, 8), :],
            send_sem=cs_sem.at[r, 2 * sx + sy], recv_sem=cr_sem.at[r, 2 * sx + sy],
            device_id=(x_at(sx), y_at(sy)), device_id_type=MESH)

    def coef_copy(toward, part):
        return pltpu.make_async_remote_copy(
            src_ref=(rate_in, coupling_in)[part], dst_ref=beside_coef.at[toward, part],
            send_sem=ks_sem.at[toward, part], recv_sem=kr_sem.at[toward, part],
            device_id=(x_at(toward), my) if toward < 2 else (me, y_at(toward - 2)), device_id_type=MESH)

    def coef_has(toward):
        return x_has[toward] if toward < 2 else y_has[toward - 2]

    def coef_from(toward):
        return x_has[1 - toward] if toward < 2 else y_has[3 - toward]

    def send_rest(r):
        for side in range(2):
            @pl.when(x_has[side])
            def _():
                x_copy(r, side).start()
        for sx, sy in both_sides:
            @pl.when(jnp.logical_and(x_has[sx], y_has[sy]))
            def _():
                corner_copy(r, sx, sy).start()

    def send_y(r):
        field = fields[2 * r]
        for i in range(cx):
            y_out[r, 0, 2 * i:2 * i + 2, :] = field[i + 2, PAD:PAD + 2, :]
            y_out[r, 1, 2 * i:2 * i + 2, :] = field[i + 2, PAD + cy - 2:PAD + cy, :]
        for side in range(2):
            @pl.when(y_has[side])
            def _():
                y_copy(r, side).start()

    def receive(r):
        field = fields[2 * r]
        for side in range(2):
            @pl.when(y_has[1 - side])
            def _():
                y_copy(r, side).wait_recv()
        for i in range(cx):
            field[i + 2, PAD - 2:PAD, :] = y_in[r, 0, 2 * i:2 * i + 2, :]
            field[i + 2, PAD + cy:PAD + cy + 2, :] = y_in[r, 1, 2 * i:2 * i + 2, :]
        for side in range(2):
            @pl.when(x_has[1 - side])
            def _():
                x_copy(r, side).wait_recv()
        for sx, sy in both_sides:
            @pl.when(jnp.logical_and(x_has[1 - sx], y_has[1 - sy]))
            def _():
                corner_copy(r, sx, sy).wait_recv()

    def sent(r):
        for side in range(2):
            @pl.when(x_has[side])
            def _():
                x_copy(r, side).wait_send()

            @pl.when(y_has[side])
            def _():
                y_copy(r, side).wait_send()
        for sx, sy in both_sides:
            @pl.when(jnp.logical_and(x_has[sx], y_has[sy]))
            def _():
                corner_copy(r, sx, sy).wait_send()

    send_rest(0)
    load.wait()
    send_y(0)
    for toward in range(4):
        @pl.when(coef_has(toward))
        def _():
            for part in range(2):
                coef_copy(toward, part).start()
    for copy in small:
        copy.wait()

    q0 = coeffs[0] - coeffs[2]
    q1 = coeffs[1] - 3.0 * coeffs[3]
    q2 = 2.0 * coeffs[2]
    q3 = 4.0 * coeffs[3]

    def columns_hit(rows, first):
        return iota((rows, cy), 0) + first == iota((rows, cy), 1)

    def spread(src, dst, i, rows, hit):
        count = hit.shape[0]
        col = jnp.sum(jnp.where(hit, jnp.broadcast_to(src, (count, cy)), 0.0), axis=1, keepdims=True)
        dst[i, rows, :] = jnp.broadcast_to(col, (count, LANES))

    def spread_own():
        def row(i, carry):
            for src, dst in ((rate, rate_b), (coupling, coup_b)):
                spread(src[pl.ds(i, 1), :], dst, i + 1, pl.ds(8, cy), columns_hit(cy, 0))
            return carry

        lax.fori_loop(0, cx, row, 0)

    def spread_beside():
        for part, dst in enumerate((rate_b, coup_b)):
            spread(beside_coef[1, part, cx - 1:cx, :], dst, 0, pl.ds(8, cy), columns_hit(cy, 0))
            spread(beside_coef[0, part, 0:1, :], dst, cx + 1, pl.ds(8, cy), columns_hit(cy, 0))

        def row(i, carry):
            for part, dst in enumerate((rate_b, coup_b)):
                spread(beside_coef[3, part, pl.ds(i, 1), :], dst, i + 1, pl.ds(0, 8), columns_hit(8, cy - 8))
                spread(beside_coef[2, part, pl.ds(i, 1), :], dst, i + 1, pl.ds(8 + cy, 8), columns_hit(8, 0))
            return carry

        lax.fori_loop(0, cx, row, 0)

    def lateral(r, i, low, high):
        old, new = fields[r], fields[r + 1]
        rows = pl.ds(PAD + low, high - low)
        beside = (old[i + 1, rows, :] + old[i + 3, rows, :]) + (
            old[i + 2, PAD - 1 + low:PAD - 1 + high, :] + old[i + 2, PAD + 1 + low:PAD + 1 + high, :])
        a = rate_b[i + 1, 8 + low:8 + high, :]
        b = coup_b[i + 1, 8 + low:8 + high, :]
        if r == 2:
            a, b = q3 * a, q3 * b
        a = jnp.concatenate([a] * reps, axis=1)
        b = jnp.concatenate([b] * reps, axis=1)
        out = a * old[i + 2, rows, :] - b * beside
        if r == 2:
            out = out + total[i + 1, 8 + low:8 + high, :]
        new[i + 2, rows, :] = out

    def inner(r, edge):
        def row(i, carry):
            lateral(r, i, 8, cy - 8)
            return carry

        lax.fori_loop(edge, cx - edge, row, 0)

    def rim(r):
        lateral(r, -1, 0, cy)
        lateral(r, cx, 0, cy)
        lateral(r, 0, -8, cy + 8)
        lateral(r, cx - 1, -8, cy + 8)

        def row(i, carry):
            lateral(r, i, -8, 8)
            lateral(r, i, cy - 8, cy + 8)
            return carry

        lax.fori_loop(1, cx - 1, row, 0)

    def rim_two(r):
        for i in (0, 1, cx - 2, cx - 1):
            lateral(r, i, 0, cy)

        def row(i, carry):
            lateral(r, i, 0, 8)
            lateral(r, i, cy - 8, cy)
            return carry

        lax.fori_loop(2, cx - 2, row, 0)

    def make_weights():
        pick = (iota((LANES, depth), 0) % depth == iota((LANES, depth), 1)).astype(F32)
        tiled = dot_t(dot_t(pick, vertical[...]), pick)
        same = iota((LANES, LANES), 0) // depth == iota((LANES, LANES), 1) // depth
        eye = jnp.where(iota((LANES, LANES), 0) == iota((LANES, LANES), 1), 1.0, 0.0)
        v1 = jnp.where(same, tiled, 0.0)
        v2 = dot(v1, v1)
        v3 = dot(v1, v2)
        polys = (
            q0 * eye + q1 * v1 + q2 * v2 + q3 * v3,
            q1 * eye + (2.0 * q2) * v1 + (3.0 * q3) * v2,
            q2 * eye + (3.0 * q3) * v1,
        )
        for k, poly in enumerate(polys):
            high, low = split2(poly)
            for row in (0, LANES):
                weights[k, row:row + LANES, 0:LANES] = high
                weights[k, row:row + LANES, LANES:2 * LANES] = low

    def depth_block(ks, i, count, low, high):
        cells = count * (high - low)
        for t in range(reps):
            lanes = slice(t * LANES, (t + 1) * LANES)
            out = None
            for k in ks:
                value = fields[k][pl.ds(i + 2, count), PAD + low:PAD + high, lanes].reshape(cells, LANES)
                both = jnp.concatenate(split2(value), axis=1)
                one = jnp.dot(both, weights[k], preferred_element_type=F32)
                out = one if out is None else out + one
            out = (out[:, 0:LANES] + out[:, LANES:2 * LANES]).reshape(count, high - low, LANES)
            spot = (pl.ds(i + 1, count), slice(8 + low, 8 + high), lanes)
            total[spot] = out if 0 in ks else total[spot] + out

    def depth_own(ks):
        def part(g, carry):
            depth_block(ks, g * GROUP, GROUP, 0, cy)
            return carry

        lax.fori_loop(0, cx // GROUP, part, 0)

    def depth_beside(ks):
        depth_block(ks, -1, 1, 0, cy)
        depth_block(ks, cx, 1, 0, cy)
        depth_block(ks, 0, cx, -8, 0)
        depth_block(ks, 0, cx, cy, cy + 8)

    hit = iota((sensors, sensors), 0) == jnp.broadcast_to(slots[...], (sensors, sensors))
    cell = jnp.sum(jnp.where(hit, jnp.broadcast_to(columns[...], (sensors, sensors)), 0), axis=1, keepdims=True)
    spots_v[...] = jnp.broadcast_to(cell, (sensors, LANES))
    to_scalars = pltpu.make_async_copy(spots_v, spots, spot_sem)
    to_scalars.start()

    spread_own()
    inner(0, 1)
    make_weights()
    for toward in range(4):
        @pl.when(coef_from(toward))
        def _():
            for part in range(2):
                coef_copy(toward, part).wait_recv()
    spread_beside()
    receive(0)
    rim(0)
    rim_two(1)
    send_rest(1)
    send_y(1)
    inner(1, 2)
    depth_own((0, 1))
    depth_own((2,))
    depth_beside((0, 1))
    inner(2, 1)
    receive(1)
    depth_beside((2,))
    rim(2)
    store = pltpu.make_async_copy(e3.at[pl.ds(2, cx), own, :], sample, store_sem)
    store.start()
    to_scalars.wait()

    def center(k, carry):
        place = spots[k, 0]
        g_c[pl.ds(k, 1), :] = e3[place // cy + 2, pl.ds(place % cy + PAD, 1), :]
        return carry

    lax.fori_loop(0, sensors, center, 0, unroll=8)
    value = g_c[...]
    mean = value[:, 0:LANES]
    for t in range(1, reps):
        mean = mean + value[:, t * LANES:(t + 1) * LANES]
    mean = (mean + pltpu.roll(mean, depth, axis=1)) * (depth / width)
    g_c[...] = (value - jnp.concatenate([mean] * reps, axis=1)) * 0.5

    parts = ready.shape[0] // sensors
    per = ready.shape[0] // n_gx
    mine = pl.ds(pl.multiple_of(me * per, per), per)

    def peer_of(i):
        far = (i + 1) // 2
        return lax.rem(me + jnp.where(i % 2 == 1, far, n_gx - far), n_gx)

    def to_peer(i):
        peer = peer_of(i)
        return pltpu.make_async_remote_copy(
            src_ref=ready.at[pl.ds(pl.multiple_of(peer * per, per), per), :], dst_ref=grads.at[mine, :],
            send_sem=as_sem.at[i], recv_sem=ar_sem.at[i], device_id=(peer, my), device_id_type=MESH)

    def blocks_for(peer):
        for m in range(sensors // n_gx):
            k = peer * (sensors // n_gx) + m
            place = spots[k, 0]
            i = place // cy
            j = place % cy + PAD
            weight = g_c[pl.ds(k, 1), :]
            along_x = weight * (e3[i + 3, pl.ds(j, 1), :] - e3[i + 1, pl.ds(j, 1), :])
            along_y = weight * (e3[i + 2, pl.ds(j + 1, 1), :] - e3[i + 2, pl.ds(j - 1, 1), :])
            for d, product in enumerate((along_x, along_y)):
                for t in range(reps):
                    ready[pl.ds(k * parts + d * reps + t, 1), :] = product[:, t * LANES:(t + 1) * LANES]

    def start(s, carry):
        i = n_gx - 1 - s
        blocks_for(peer_of(i))
        to_peer(i).start()
        return carry

    lax.fori_loop(0, n_gx - 1, start, 0)
    blocks_for(me)
    keep = pltpu.make_async_copy(ready.at[mine, :], grads.at[mine, :], own_sem)
    keep.start()
    for r in range(2):
        sent(r)
    for toward in range(4):
        @pl.when(coef_has(toward))
        def _():
            for part in range(2):
                coef_copy(toward, part).wait_send()
    store.wait()
    keep.wait()

    def finish(i, carry):
        copy = to_peer(i)
        copy.wait_send()
        copy.wait_recv()
        return carry

    lax.fori_loop(1, n_gx, finish, 0)


def finish_kernel(sample_in, grads_in, sample, grads, flat, rows, in_sem, out_sem, load_sem, store_sem, whole):
    sensors, parts = rows.shape[0], rows.shape[1] // LANES
    first = pltpu.make_async_copy(grads_in, flat, in_sem)
    first.start()
    cut = sample.shape[0] // 4
    spots = [pl.ds(p * cut, cut) for p in range(4)]
    loads = [pltpu.make_async_copy(sample_in.at[s], whole.at[s], load_sem.at[p]) for p, s in enumerate(spots)]
    stores = [pltpu.make_async_copy(whole.at[s], sample.at[s], store_sem.at[p]) for p, s in enumerate(spots)]
    for copy in loads:
        copy.start()
    first.wait()
    for t in range(parts):
        rows[:, t * LANES:(t + 1) * LANES] = flat[pl.ds(t, sensors, stride=parts), :]
    last = pltpu.make_async_copy(rows, grads, out_sem)
    last.start()
    for load, store in zip(loads, stores):
        load.wait()
        store.start()
    for store in stores:
        store.wait()
    last.wait()


def shards(n_gx, n_gy, noise, rate, coupling, vertical, coeffs, columns, slots):
    cx, cy, width = noise.shape
    sensors = slots.shape[1]
    parts = 2 * width // LANES
    hbm = pl.BlockSpec(memory_space=pltpu.HBM)
    field = pltpu.VMEM((cx + 4, cy + 2 * PAD, width), F32)
    coef = pltpu.VMEM((cx + 2, cy + 16, LANES), F32)
    dma = pltpu.SemaphoreType.DMA
    sample, grads = pl.pallas_call(
        functools.partial(kernel, n_gx, n_gy),
        out_shape=(jax.ShapeDtypeStruct(noise.shape, F32),
                   jax.ShapeDtypeStruct((sensors * parts, LANES), F32)),
        in_specs=[hbm] * 7,
        out_specs=(hbm, hbm),
        scratch_shapes=[
            pltpu.VMEM(rate.shape, F32), pltpu.VMEM(coupling.shape, F32), pltpu.VMEM(vertical.shape, F32),
            pltpu.VMEM(slots.shape, jnp.int32), pltpu.VMEM(columns.shape, jnp.int32), pltpu.SMEM(coeffs.shape, F32),
            field, field, field, field, pltpu.VMEM((cx + 2, cy + 16, width), F32),
            coef, coef,
            pltpu.VMEM((3, 2 * LANES, 2 * LANES), BF16),
            pltpu.VMEM((2, 2, 2 * cx, width), F32), pltpu.VMEM((2, 2, 2 * cx, width), F32),
            pltpu.VMEM((4, 2, cx, cy), F32),
            pltpu.VMEM((sensors, LANES), jnp.int32), pltpu.SMEM((sensors, LANES), jnp.int32),
            pltpu.VMEM((sensors, width), F32), pltpu.VMEM((sensors * parts, LANES), F32),
            dma((6,)), dma, dma((2, 2)), dma((2, 2)), dma((2, 2)), dma((2, 2)),
            dma((2, 4)), dma((2, 4)), dma((4, 2)), dma((4, 2)),
            dma((n_gx,)), dma((n_gx,)), dma, dma, dma,
        ],
        compiler_params=pltpu.CompilerParams(
            collective_id=0, has_side_effects=True, vmem_limit_bytes=61 << 20),
    )(noise, rate, coupling, vertical, slots, columns, coeffs)
    return pl.pallas_call(
        finish_kernel,
        out_shape=(jax.ShapeDtypeStruct(noise.shape, F32),
                   jax.ShapeDtypeStruct((sensors, parts * LANES), F32)),
        in_specs=[pl.BlockSpec(memory_space=pl.ANY)] * 2,
        out_specs=(hbm, hbm),
        scratch_shapes=[
            pltpu.VMEM((sensors * parts, LANES), F32), pltpu.VMEM((sensors, parts * LANES), F32),
            dma, dma, dma((4,)), dma((4,)), pltpu.VMEM(noise.shape, F32),
        ],
        compiler_params=pltpu.CompilerParams(vmem_limit_bytes=61 << 20),
    )(sample, grads)


def solution(mesh):
    placed = (
        P("gx", "gy", None),
        P("gx", "gy"),
        P("gx", "gy"),
        P(),
        P(),
        P(("gx", "gy"), None),
        P(("gx", "gy"), None),
    )
    return jax.shard_map(
        functools.partial(shards, mesh.shape["gx"], mesh.shape["gy"]),
        mesh=mesh,
        in_specs=placed,
        out_specs=(P("gx", "gy", None), P(("gx", "gy"), None)),
        check_vma=False,
    )
```

```python
import functools

import jax
import jax.numpy as jnp
from jax import lax
from jax.experimental import pallas as pl
from jax.experimental.pallas import tpu as pltpu
from jax.sharding import PartitionSpec as P

MESH = pl.DeviceIdType.MESH
HIGHEST = lax.Precision.HIGHEST
F32 = jnp.float32
BF16 = jnp.bfloat16
LANES = 128
GROUP = 4
BATCH = 4
PAD = 16


def split2(value):
    high = value.astype(BF16)
    return high, (value - high.astype(F32)).astype(BF16)


def iota(shape, dim):
    return lax.broadcasted_iota(jnp.int32, shape, dim)


def dot_t(a, b):
    return lax.dot_general(a, b, (((1,), (1,)), ((), ())), precision=HIGHEST, preferred_element_type=F32)


def dot(a, b):
    return jnp.dot(a, b, precision=HIGHEST, preferred_element_type=F32)


def kernel(n_gx, n_gy, noise, rate_in, coupling_in, vertical_in, slots_in, columns_in, coeffs_in, sample, grads,
           rate, coupling, vertical, slots, columns, coeffs, e0, e1, e2, e3, total, rate_b, coup_b, weights,
           y_out, y_in, beside_coef, spots_v, spots, g_c, ready,
           small_sem, load_sem, xs_sem, xr_sem, ys_sem, yr_sem, cs_sem, cr_sem, ks_sem, kr_sem, as_sem, ar_sem, store_sem, own_sem, spot_sem):
    cx, cy, width = noise.shape
    depth = vertical.shape[0]
    sensors = slots.shape[1]
    reps = width // LANES
    me = lax.axis_index("gx")
    my = lax.axis_index("gy")
    fields = (e0, e1, e2, e3)
    own = pl.ds(PAD, cy)
    x_has = (me > 0, me < n_gx - 1)
    y_has = (my > 0, my < n_gy - 1)
    both_sides = [(sx, sy) for sx in range(2) for sy in range(2)]

    def x_at(side):
        return me - 1 if side == 0 else me + 1

    def y_at(side):
        return my - 1 if side == 0 else my + 1

    def peer_of(i):
        far = (i + 1) // 2
        return lax.rem(me + jnp.where(i % 2 == 1, far, n_gx - far), n_gx)

    barrier = pltpu.get_barrier_semaphore()

    beside_y = [(y_has[sy], (me, y_at(sy))) for sy in range(2)]
    beside_y += [(jnp.logical_and(x_has[sx], y_has[sy]), (x_at(sx), y_at(sy))) for sx, sy in both_sides]
    arrivals = n_gx - 1
    for there, device in beside_y:
        arrivals = arrivals + jnp.where(there, 1, 0)

        @pl.when(there)
        def _():
            pl.semaphore_signal(barrier, inc=1, device_id=device, device_id_type=MESH)

    def greet(s, carry):
        pl.semaphore_signal(barrier, inc=1, device_id=(peer_of(n_gx - 1 - s), my), device_id_type=MESH)
        return carry

    lax.fori_loop(0, n_gx - 1, greet, 0)
    loads = [
        pltpu.make_async_copy(noise.at[:, pl.ds(low, count), :], e0.at[pl.ds(2, cx), pl.ds(PAD + low, count), :], load_sem.at[i])
        for i, (low, count) in enumerate(((0, 8), (cy - 8, 8), (8, cy - 16)))
    ]
    for copy in loads:
        copy.start()
    small = [
        pltpu.make_async_copy(src, dst, small_sem.at[i])
        for i, (src, dst) in enumerate((
            (rate_in, rate), (coupling_in, coupling), (vertical_in, vertical),
            (slots_in, slots), (columns_in, columns), (coeffs_in, coeffs)))
    ]
    for copy in small:
        copy.start()

    for side in range(2):
        @pl.when(jnp.logical_not(x_has[side]))
        def _():
            for field in (e0, e2):
                for i in (0, 1) if side == 0 else (cx + 2, cx + 3):
                    field[i] = jnp.zeros(field.shape[1:], F32)
            beside_coef[1 - side] = jnp.zeros(beside_coef.shape[1:], F32)

        @pl.when(jnp.logical_not(y_has[side]))
        def _():
            for field in (e0, e2):
                for i in (1, cx + 2):
                    block = pl.ds(PAD - 8 if side == 0 else PAD + cy, 8)
                    field[i, block, :] = jnp.zeros((8, width), F32)
            for r in range(2):
                y_in[r, side] = jnp.zeros(y_in.shape[2:], F32)
            beside_coef[3 - side] = jnp.zeros(beside_coef.shape[1:], F32)

    pl.semaphore_wait(barrier, arrivals)

    def x_copy(r, side):
        field = fields[2 * r]
        row = 0 if side == 0 else cx - 2
        src = noise.at[pl.ds(row, 2)] if r == 0 else field.at[pl.ds(row + 2, 2), own, :]
        return pltpu.make_async_remote_copy(
            src_ref=src, dst_ref=field.at[pl.ds(cx + 2 if side == 0 else 0, 2), own, :],
            send_sem=xs_sem.at[r, side], recv_sem=xr_sem.at[r, side],
            device_id=(x_at(side), my), device_id_type=MESH)

    def y_copy(r, side):
        return pltpu.make_async_remote_copy(
            src_ref=y_out.at[r, side], dst_ref=y_in.at[r, 1 - side],
            send_sem=ys_sem.at[r, side], recv_sem=yr_sem.at[r, side],
            device_id=(me, y_at(side)), device_id_type=MESH)

    def corner_copy(r, sx, sy):
        field = fields[2 * r]
        row = 0 if sx == 0 else cx - 1
        col = 0 if sy == 0 else cy - 8
        src = noise.at[row, pl.ds(col, 8), :] if r == 0 else field.at[row + 2, pl.ds(PAD + col, 8), :]
        return pltpu.make_async_remote_copy(
            src_ref=src, dst_ref=field.at[cx + 2 if sx == 0 else 1, pl.ds(PAD + cy if sy == 0 else PAD - 8, 8), :],
            send_sem=cs_sem.at[r, 2 * sx + sy], recv_sem=cr_sem.at[r, 2 * sx + sy],
            device_id=(x_at(sx), y_at(sy)), device_id_type=MESH)

    def coef_copy(toward, part):
        return pltpu.make_async_remote_copy(
            src_ref=(rate_in, coupling_in)[part], dst_ref=beside_coef.at[toward, part],
            send_sem=ks_sem.at[toward, part], recv_sem=kr_sem.at[toward, part],
            device_id=(x_at(toward), my) if toward < 2 else (me, y_at(toward - 2)), device_id_type=MESH)

    def coef_has(toward):
        return x_has[toward] if toward < 2 else y_has[toward - 2]

    def coef_from(toward):
        return x_has[1 - toward] if toward < 2 else y_has[3 - toward]

    def send_rest(r):
        for side in range(2):
            @pl.when(x_has[side])
            def _():
                x_copy(r, side).start()
        for sx, sy in both_sides:
            @pl.when(jnp.logical_and(x_has[sx], y_has[sy]))
            def _():
                corner_copy(r, sx, sy).start()

    def send_y(r):
        field = fields[2 * r]
        for i in range(cx):
            y_out[r, 0, 2 * i:2 * i + 2, :] = field[i + 2, PAD:PAD + 2, :]
            y_out[r, 1, 2 * i:2 * i + 2, :] = field[i + 2, PAD + cy - 2:PAD + cy, :]
        for side in range(2):
            @pl.when(y_has[side])
            def _():
                y_copy(r, side).start()

    def receive(r):
        field = fields[2 * r]
        for side in range(2):
            @pl.when(y_has[1 - side])
            def _():
                y_copy(r, side).wait_recv()
        for i in range(cx):
            field[i + 2, PAD - 2:PAD, :] = y_in[r, 0, 2 * i:2 * i + 2, :]
            field[i + 2, PAD + cy:PAD + cy + 2, :] = y_in[r, 1, 2 * i:2 * i + 2, :]
        for side in range(2):
            @pl.when(x_has[1 - side])
            def _():
                x_copy(r, side).wait_recv()
        for sx, sy in both_sides:
            @pl.when(jnp.logical_and(x_has[1 - sx], y_has[1 - sy]))
            def _():
                corner_copy(r, sx, sy).wait_recv()

    def sent(r):
        for side in range(2):
            @pl.when(x_has[side])
            def _():
                x_copy(r, side).wait_send()

            @pl.when(y_has[side])
            def _():
                y_copy(r, side).wait_send()
        for sx, sy in both_sides:
            @pl.when(jnp.logical_and(x_has[sx], y_has[sy]))
            def _():
                corner_copy(r, sx, sy).wait_send()

    send_rest(0)
    loads[0].wait()
    loads[1].wait()
    send_y(0)
    for toward in range(4):
        @pl.when(coef_has(toward))
        def _():
            for part in range(2):
                coef_copy(toward, part).start()
    for copy in small:
        copy.wait()
    loads[2].wait()

    q0 = coeffs[0] - coeffs[2]
    q1 = coeffs[1] - 3.0 * coeffs[3]
    q2 = 2.0 * coeffs[2]
    q3 = 4.0 * coeffs[3]

    def columns_hit(rows, first):
        return iota((rows, cy), 0) + first == iota((rows, cy), 1)

    def spread(src, dst, i, rows, hit):
        count = hit.shape[0]
        col = jnp.sum(jnp.where(hit, jnp.broadcast_to(src, (count, cy)), 0.0), axis=1, keepdims=True)
        dst[i, rows, :] = jnp.broadcast_to(col, (count, LANES))

    def spread_own():
        def row(i, carry):
            for src, dst in ((rate, rate_b), (coupling, coup_b)):
                spread(src[pl.ds(i, 1), :], dst, i + 1, pl.ds(8, cy), columns_hit(cy, 0))
            return carry

        lax.fori_loop(0, cx, row, 0)

    def spread_beside():
        for part, dst in enumerate((rate_b, coup_b)):
            spread(beside_coef[1, part, cx - 1:cx, :], dst, 0, pl.ds(8, cy), columns_hit(cy, 0))
            spread(beside_coef[0, part, 0:1, :], dst, cx + 1, pl.ds(8, cy), columns_hit(cy, 0))

        def row(i, carry):
            for part, dst in enumerate((rate_b, coup_b)):
                spread(beside_coef[3, part, pl.ds(i, 1), :], dst, i + 1, pl.ds(0, 8), columns_hit(8, cy - 8))
                spread(beside_coef[2, part, pl.ds(i, 1), :], dst, i + 1, pl.ds(8 + cy, 8), columns_hit(8, 0))
            return carry

        lax.fori_loop(0, cx, row, 0)

    def lateral(r, i, low, high):
        old, new = fields[r], fields[r + 1]
        rows = pl.ds(PAD + low, high - low)
        beside = (old[i + 1, rows, :] + old[i + 3, rows, :]) + (
            old[i + 2, PAD - 1 + low:PAD - 1 + high, :] + old[i + 2, PAD + 1 + low:PAD + 1 + high, :])
        a = rate_b[i + 1, 8 + low:8 + high, :]
        b = coup_b[i + 1, 8 + low:8 + high, :]
        if r == 2:
            a, b = q3 * a, q3 * b
        a = jnp.concatenate([a] * reps, axis=1)
        b = jnp.concatenate([b] * reps, axis=1)
        out = a * old[i + 2, rows, :] - b * beside
        if r == 2:
            out = out + total[i + 1, 8 + low:8 + high, :]
        new[i + 2, rows, :] = out

    def inner(r, edge):
        def row(i, carry):
            lateral(r, i, 8, cy - 8)
            return carry

        lax.fori_loop(edge, cx - edge, row, 0)

    def rim(r):
        lateral(r, -1, 0, cy)
        lateral(r, cx, 0, cy)
        lateral(r, 0, -8, cy + 8)
        lateral(r, cx - 1, -8, cy + 8)

        def row(i, carry):
            lateral(r, i, -8, 8)
            lateral(r, i, cy - 8, cy + 8)
            return carry

        lax.fori_loop(1, cx - 1, row, 0)

    def rim_two(r):
        for i in (0, 1, cx - 2, cx - 1):
            lateral(r, i, 0, cy)

        def row(i, carry):
            lateral(r, i, 0, 8)
            lateral(r, i, cy - 8, cy)
            return carry

        lax.fori_loop(2, cx - 2, row, 0)

    def make_weights():
        pick = (iota((LANES, depth), 0) % depth == iota((LANES, depth), 1)).astype(F32)
        tiled = dot_t(dot_t(pick, vertical[...]), pick)
        same = iota((LANES, LANES), 0) // depth == iota((LANES, LANES), 1) // depth
        eye = jnp.where(iota((LANES, LANES), 0) == iota((LANES, LANES), 1), 1.0, 0.0)
        v1 = jnp.where(same, tiled, 0.0)
        v2 = dot(v1, v1)
        v3 = dot(v1, v2)
        polys = (
            q0 * eye + q1 * v1 + q2 * v2 + q3 * v3,
            q1 * eye + (2.0 * q2) * v1 + (3.0 * q3) * v2,
            q2 * eye + (3.0 * q3) * v1,
        )
        for k, poly in enumerate(polys):
            high, low = split2(poly)
            for row in (0, LANES):
                weights[k, row:row + LANES, 0:LANES] = high
                weights[k, row:row + LANES, LANES:2 * LANES] = low

    def depth_block(ks, i, count, low, high):
        cells = count * (high - low)
        for t in range(reps):
            lanes = slice(t * LANES, (t + 1) * LANES)
            out = None
            for k in ks:
                value = fields[k][pl.ds(i + 2, count), PAD + low:PAD + high, lanes].reshape(cells, LANES)
                both = jnp.concatenate(split2(value), axis=1)
                one = jnp.dot(both, weights[k], preferred_element_type=F32)
                out = one if out is None else out + one
            out = (out[:, 0:LANES] + out[:, LANES:2 * LANES]).reshape(count, high - low, LANES)
            spot = (pl.ds(i + 1, count), slice(8 + low, 8 + high), lanes)
            total[spot] = out if 0 in ks else total[spot] + out

    def depth_own(ks):
        def part(g, carry):
            depth_block(ks, g * GROUP, GROUP, 0, cy)
            return carry

        lax.fori_loop(0, cx // GROUP, part, 0)

    def depth_beside(ks):
        depth_block(ks, -1, 1, 0, cy)
        depth_block(ks, cx, 1, 0, cy)
        depth_block(ks, 0, cx, -8, 0)
        depth_block(ks, 0, cx, cy, cy + 8)

    hit = iota((sensors, sensors), 0) == jnp.broadcast_to(slots[...], (sensors, sensors))
    cell = jnp.sum(jnp.where(hit, jnp.broadcast_to(columns[...], (sensors, sensors)), 0), axis=1, keepdims=True)
    spots_v[...] = jnp.broadcast_to(cell, (sensors, LANES))
    to_scalars = pltpu.make_async_copy(spots_v, spots, spot_sem)
    to_scalars.start()

    spread_own()
    inner(0, 1)
    make_weights()
    depth_own((0,))
    for toward in range(4):
        @pl.when(coef_from(toward))
        def _():
            for part in range(2):
                coef_copy(toward, part).wait_recv()
    spread_beside()
    receive(0)
    rim(0)
    rim_two(1)
    send_rest(1)
    send_y(1)
    inner(1, 2)
    depth_own((1,))
    depth_own((2,))
    depth_beside((0, 1))
    inner(2, 1)
    receive(1)
    depth_beside((2,))
    rim(2)
    store = pltpu.make_async_copy(e3.at[pl.ds(2, cx), own, :], sample, store_sem)
    store.start()
    to_scalars.wait()

    def center(k, carry):
        place = spots[k, 0]
        g_c[pl.ds(k, 1), :] = e3[place // cy + 2, pl.ds(place % cy + PAD, 1), :]
        return carry

    lax.fori_loop(0, sensors, center, 0, unroll=8)
    value = g_c[...]
    mean = value[:, 0:LANES]
    for t in range(1, reps):
        mean = mean + value[:, t * LANES:(t + 1) * LANES]
    mean = (mean + pltpu.roll(mean, depth, axis=1)) * (depth / width)
    g_c[...] = (value - jnp.concatenate([mean] * reps, axis=1)) * 0.5

    parts = ready.shape[0] // sensors
    per = ready.shape[0] // n_gx
    mine = pl.ds(pl.multiple_of(me * per, per), per)

    def to_peer(i):
        peer = peer_of(i)
        return pltpu.make_async_remote_copy(
            src_ref=ready.at[pl.ds(pl.multiple_of(peer * per, per), per), :], dst_ref=grads.at[mine, :],
            send_sem=as_sem.at[i], recv_sem=ar_sem.at[i], device_id=(peer, my), device_id_type=MESH)

    def blocks_for(peer):
        for m in range(sensors // n_gx):
            k = peer * (sensors // n_gx) + m
            place = spots[k, 0]
            i = place // cy
            j = place % cy + PAD
            weight = g_c[pl.ds(k, 1), :]
            along_x = weight * (e3[i + 3, pl.ds(j, 1), :] - e3[i + 1, pl.ds(j, 1), :])
            along_y = weight * (e3[i + 2, pl.ds(j + 1, 1), :] - e3[i + 2, pl.ds(j - 1, 1), :])
            for d, product in enumerate((along_x, along_y)):
                for t in range(reps):
                    ready[pl.ds(k * parts + d * reps + t, 1), :] = product[:, t * LANES:(t + 1) * LANES]

    batch = BATCH if n_gx % BATCH == 0 else 1

    def start(g, carry):
        turns = [1 + g * batch + b for b in range(batch)]
        for i in turns:
            blocks_for(peer_of(i))
        for i in turns:
            to_peer(i).start()
        return carry

    lax.fori_loop(0, n_gx // batch - 1, start, 0)
    for i in list(range(n_gx - batch + 1, n_gx)) + [0]:
        blocks_for(peer_of(i))
    for i in range(n_gx - batch + 1, n_gx):
        to_peer(i).start()
    keep = pltpu.make_async_copy(ready.at[mine, :], grads.at[mine, :], own_sem)
    keep.start()
    for r in range(2):
        sent(r)
    for toward in range(4):
        @pl.when(coef_has(toward))
        def _():
            for part in range(2):
                coef_copy(toward, part).wait_send()
    store.wait()
    keep.wait()

    def finish(i, carry):
        copy = to_peer(i)
        copy.wait_send()
        copy.wait_recv()
        return carry

    lax.fori_loop(1, n_gx, finish, 0)


def finish_kernel(sample_in, grads_in, sample, grads, rows, out_sem, store_sem):
    sensors, parts = rows.shape[0], rows.shape[1] // LANES
    cut = sample.shape[0] // 4
    spots = [pl.ds(p * cut, cut) for p in range(4)]
    stores = [pltpu.make_async_copy(sample_in.at[s], sample.at[s], store_sem.at[p]) for p, s in enumerate(spots)]
    for copy in stores:
        copy.start()
    for t in range(parts):
        rows[:, t * LANES:(t + 1) * LANES] = grads_in[pl.ds(t, sensors, stride=parts), :]
    last = pltpu.make_async_copy(rows, grads, out_sem)
    last.start()
    for store in stores:
        store.wait()
    last.wait()


def shards(n_gx, n_gy, noise, rate, coupling, vertical, coeffs, columns, slots):
    cx, cy, width = noise.shape
    sensors = slots.shape[1]
    parts = 2 * width // LANES
    hbm = pl.BlockSpec(memory_space=pltpu.HBM)
    vmem = pl.BlockSpec(memory_space=pltpu.VMEM)
    field = pltpu.VMEM((cx + 4, cy + 2 * PAD, width), F32)
    coef = pltpu.VMEM((cx + 2, cy + 16, LANES), F32)
    dma = pltpu.SemaphoreType.DMA
    sample, grads = pl.pallas_call(
        functools.partial(kernel, n_gx, n_gy),
        out_shape=(pltpu.VMEM(noise.shape, F32), pltpu.VMEM((sensors * parts, LANES), F32)),
        in_specs=[hbm] * 7,
        out_specs=(vmem, vmem),
        scratch_shapes=[
            pltpu.VMEM(rate.shape, F32), pltpu.VMEM(coupling.shape, F32), pltpu.VMEM(vertical.shape, F32),
            pltpu.VMEM(slots.shape, jnp.int32), pltpu.VMEM(columns.shape, jnp.int32), pltpu.SMEM(coeffs.shape, F32),
            field, field, field, field, pltpu.VMEM((cx + 2, cy + 16, width), F32),
            coef, coef,
            pltpu.VMEM((3, 2 * LANES, 2 * LANES), BF16),
            pltpu.VMEM((2, 2, 2 * cx, width), F32), pltpu.VMEM((2, 2, 2 * cx, width), F32),
            pltpu.VMEM((4, 2, cx, cy), F32),
            pltpu.VMEM((sensors, LANES), jnp.int32), pltpu.SMEM((sensors, LANES), jnp.int32),
            pltpu.VMEM((sensors, width), F32), pltpu.VMEM((sensors * parts, LANES), F32),
            dma((6,)), dma((3,)), dma((2, 2)), dma((2, 2)), dma((2, 2)), dma((2, 2)),
            dma((2, 4)), dma((2, 4)), dma((4, 2)), dma((4, 2)),
            dma((n_gx,)), dma((n_gx,)), dma, dma, dma,
        ],
        compiler_params=pltpu.CompilerParams(
            collective_id=0, has_side_effects=True, vmem_limit_bytes=56 << 20),
    )(*(pltpu.with_memory_space_constraint(arg, pltpu.HBM)
        for arg in (noise, rate, coupling, vertical, slots, columns, coeffs)))
    return pl.pallas_call(
        finish_kernel,
        out_shape=(jax.ShapeDtypeStruct(noise.shape, F32),
                   jax.ShapeDtypeStruct((sensors, parts * LANES), F32)),
        in_specs=[pl.BlockSpec(memory_space=pltpu.VMEM)] * 2,
        out_specs=(hbm, hbm),
        scratch_shapes=[
            pltpu.VMEM((sensors, parts * LANES), F32), dma, dma((4,)),
        ],
        compiler_params=pltpu.CompilerParams(vmem_limit_bytes=16 << 20),
    )(sample, grads)


def solution(mesh):
    placed = (
        P("gx", "gy", None),
        P("gx", "gy"),
        P("gx", "gy"),
        P(),
        P(),
        P(("gx", "gy"), None),
        P(("gx", "gy"), None),
    )
    return jax.shard_map(
        functools.partial(shards, mesh.shape["gx"], mesh.shape["gy"]),
        mesh=mesh,
        in_specs=placed,
        out_specs=(P("gx", "gy", None), P(("gx", "gy"), None)),
        check_vma=False,
    )
```

```python
import functools

import jax
import jax.numpy as jnp
from jax import lax
from jax.experimental import pallas as pl
from jax.experimental.pallas import tpu as pltpu
from jax.sharding import PartitionSpec as P

MESH = pl.DeviceIdType.MESH
HIGHEST = lax.Precision.HIGHEST
F32 = jnp.float32
BF16 = jnp.bfloat16
LANES = 128
GROUP = 4
BATCH = 4
PAD = 16


def split2(value):
    high = value.astype(BF16)
    return high, (value - high.astype(F32)).astype(BF16)


def iota(shape, dim):
    return lax.broadcasted_iota(jnp.int32, shape, dim)


def dot_t(a, b):
    return lax.dot_general(a, b, (((1,), (1,)), ((), ())), precision=HIGHEST, preferred_element_type=F32)


def dot(a, b):
    return jnp.dot(a, b, precision=HIGHEST, preferred_element_type=F32)


def kernel(n_gx, n_gy, noise, rate_in, coupling_in, vertical_in, slots_in, columns_in, coeffs_in, sample, grads,
           rate, coupling, vertical, slots, columns, coeffs, e0, e1, e2, e3, total, rate_b, coup_b, weights,
           y_out, y_in, beside_coef, spots_v, spots, ready,
           small_sem, load_sem, xs_sem, xr_sem, ys_sem, yr_sem, cs_sem, cr_sem, ks_sem, kr_sem, as_sem, ar_sem, store_sem, own_sem, spot_sem):
    cx, cy, width = noise.shape
    depth = vertical.shape[0]
    sensors = slots.shape[1]
    reps = width // LANES
    me = lax.axis_index("gx")
    my = lax.axis_index("gy")
    fields = (e0, e1, e2, e3)
    own = pl.ds(PAD, cy)
    x_has = (me > 0, me < n_gx - 1)
    y_has = (my > 0, my < n_gy - 1)
    both_sides = [(sx, sy) for sx in range(2) for sy in range(2)]

    def x_at(side):
        return me - 1 if side == 0 else me + 1

    def y_at(side):
        return my - 1 if side == 0 else my + 1

    def peer_of(i):
        far = (i + 1) // 2
        return lax.rem(me + jnp.where(i % 2 == 1, far, n_gx - far), n_gx)

    barrier = pltpu.get_barrier_semaphore()

    beside_y = [(y_has[sy], (me, y_at(sy))) for sy in range(2)]
    beside_y += [(jnp.logical_and(x_has[sx], y_has[sy]), (x_at(sx), y_at(sy))) for sx, sy in both_sides]
    arrivals = n_gx - 1
    for there, device in beside_y:
        arrivals = arrivals + jnp.where(there, 1, 0)

        @pl.when(there)
        def _():
            pl.semaphore_signal(barrier, inc=1, device_id=device, device_id_type=MESH)

    def greet(s, carry):
        pl.semaphore_signal(barrier, inc=1, device_id=(peer_of(n_gx - 1 - s), my), device_id_type=MESH)
        return carry

    lax.fori_loop(0, n_gx - 1, greet, 0)
    loads = [
        pltpu.make_async_copy(noise.at[:, pl.ds(low, count), :], e0.at[pl.ds(2, cx), pl.ds(PAD + low, count), :], load_sem.at[i])
        for i, (low, count) in enumerate(((0, 8), (cy - 8, 8), (8, cy - 16)))
    ]
    for copy in loads:
        copy.start()
    small = [
        pltpu.make_async_copy(src, dst, small_sem.at[i])
        for i, (src, dst) in enumerate((
            (rate_in, rate), (coupling_in, coupling), (vertical_in, vertical),
            (slots_in, slots), (columns_in, columns), (coeffs_in, coeffs)))
    ]
    for copy in small:
        copy.start()

    for side in range(2):
        @pl.when(jnp.logical_not(x_has[side]))
        def _():
            for field in (e0, e2):
                for i in (0, 1) if side == 0 else (cx + 2, cx + 3):
                    field[i] = jnp.zeros(field.shape[1:], F32)
            beside_coef[1 - side] = jnp.zeros(beside_coef.shape[1:], F32)

        @pl.when(jnp.logical_not(y_has[side]))
        def _():
            for field in (e0, e2):
                for i in (1, cx + 2):
                    block = pl.ds(PAD - 8 if side == 0 else PAD + cy, 8)
                    field[i, block, :] = jnp.zeros((8, width), F32)
            for r in range(2):
                y_in[r, side] = jnp.zeros(y_in.shape[2:], F32)
            beside_coef[3 - side] = jnp.zeros(beside_coef.shape[1:], F32)

    pl.semaphore_wait(barrier, arrivals)

    def x_copy(r, side):
        field = fields[2 * r]
        row = 0 if side == 0 else cx - 2
        src = noise.at[pl.ds(row, 2)] if r == 0 else field.at[pl.ds(row + 2, 2), own, :]
        return pltpu.make_async_remote_copy(
            src_ref=src, dst_ref=field.at[pl.ds(cx + 2 if side == 0 else 0, 2), own, :],
            send_sem=xs_sem.at[r, side], recv_sem=xr_sem.at[r, side],
            device_id=(x_at(side), my), device_id_type=MESH)

    def y_copy(r, side):
        return pltpu.make_async_remote_copy(
            src_ref=y_out.at[r, side], dst_ref=y_in.at[r, 1 - side],
            send_sem=ys_sem.at[r, side], recv_sem=yr_sem.at[r, side],
            device_id=(me, y_at(side)), device_id_type=MESH)

    def corner_copy(r, sx, sy):
        field = fields[2 * r]
        row = 0 if sx == 0 else cx - 1
        col = 0 if sy == 0 else cy - 8
        src = noise.at[row, pl.ds(col, 8), :] if r == 0 else field.at[row + 2, pl.ds(PAD + col, 8), :]
        return pltpu.make_async_remote_copy(
            src_ref=src, dst_ref=field.at[cx + 2 if sx == 0 else 1, pl.ds(PAD + cy if sy == 0 else PAD - 8, 8), :],
            send_sem=cs_sem.at[r, 2 * sx + sy], recv_sem=cr_sem.at[r, 2 * sx + sy],
            device_id=(x_at(sx), y_at(sy)), device_id_type=MESH)

    def coef_copy(toward, part):
        return pltpu.make_async_remote_copy(
            src_ref=(rate_in, coupling_in)[part], dst_ref=beside_coef.at[toward, part],
            send_sem=ks_sem.at[toward, part], recv_sem=kr_sem.at[toward, part],
            device_id=(x_at(toward), my) if toward < 2 else (me, y_at(toward - 2)), device_id_type=MESH)

    def coef_has(toward):
        return x_has[toward] if toward < 2 else y_has[toward - 2]

    def coef_from(toward):
        return x_has[1 - toward] if toward < 2 else y_has[3 - toward]

    def send_corners(r):
        for sx, sy in both_sides:
            @pl.when(jnp.logical_and(x_has[sx], y_has[sy]))
            def _():
                corner_copy(r, sx, sy).start()

    def send_x(r):
        for side in range(2):
            @pl.when(x_has[side])
            def _():
                x_copy(r, side).start()

    def send_y(r):
        field = fields[2 * r]
        for i in range(cx):
            y_out[r, 0, 2 * i:2 * i + 2, :] = field[i + 2, PAD:PAD + 2, :]
            y_out[r, 1, 2 * i:2 * i + 2, :] = field[i + 2, PAD + cy - 2:PAD + cy, :]
        for side in range(2):
            @pl.when(y_has[side])
            def _():
                y_copy(r, side).start()

    def receive(r):
        field = fields[2 * r]
        for side in range(2):
            @pl.when(y_has[1 - side])
            def _():
                y_copy(r, side).wait_recv()
        for i in range(cx):
            field[i + 2, PAD - 2:PAD, :] = y_in[r, 0, 2 * i:2 * i + 2, :]
            field[i + 2, PAD + cy:PAD + cy + 2, :] = y_in[r, 1, 2 * i:2 * i + 2, :]
        for side in range(2):
            @pl.when(x_has[1 - side])
            def _():
                x_copy(r, side).wait_recv()
        for sx, sy in both_sides:
            @pl.when(jnp.logical_and(x_has[1 - sx], y_has[1 - sy]))
            def _():
                corner_copy(r, sx, sy).wait_recv()

    def sent(r):
        for side in range(2):
            @pl.when(x_has[side])
            def _():
                x_copy(r, side).wait_send()

            @pl.when(y_has[side])
            def _():
                y_copy(r, side).wait_send()
        for sx, sy in both_sides:
            @pl.when(jnp.logical_and(x_has[sx], y_has[sy]))
            def _():
                corner_copy(r, sx, sy).wait_send()

    send_corners(0)
    for toward in range(4):
        @pl.when(coef_has(toward))
        def _():
            for part in range(2):
                coef_copy(toward, part).start()
    loads[0].wait()
    loads[1].wait()
    send_y(0)
    send_x(0)
    for copy in small:
        copy.wait()
    loads[2].wait()

    q0 = coeffs[0] - coeffs[2]
    q1 = coeffs[1] - 3.0 * coeffs[3]
    q2 = 2.0 * coeffs[2]
    q3 = 4.0 * coeffs[3]

    def columns_hit(rows, first):
        return iota((rows, cy), 0) + first == iota((rows, cy), 1)

    def spread(src, dst, i, rows, hit):
        count = hit.shape[0]
        col = jnp.sum(jnp.where(hit, jnp.broadcast_to(src, (count, cy)), 0.0), axis=1, keepdims=True)
        dst[i, rows, :] = jnp.broadcast_to(col, (count, LANES))

    def spread_own():
        def row(i, carry):
            for src, dst in ((rate, rate_b), (coupling, coup_b)):
                spread(src[pl.ds(i, 1), :], dst, i + 1, pl.ds(8, cy), columns_hit(cy, 0))
            return carry

        lax.fori_loop(0, cx, row, 0)

    def spread_beside():
        for part, dst in enumerate((rate_b, coup_b)):
            spread(beside_coef[1, part, cx - 1:cx, :], dst, 0, pl.ds(8, cy), columns_hit(cy, 0))
            spread(beside_coef[0, part, 0:1, :], dst, cx + 1, pl.ds(8, cy), columns_hit(cy, 0))

        def row(i, carry):
            for part, dst in enumerate((rate_b, coup_b)):
                spread(beside_coef[3, part, pl.ds(i, 1), :], dst, i + 1, pl.ds(0, 8), columns_hit(8, cy - 8))
                spread(beside_coef[2, part, pl.ds(i, 1), :], dst, i + 1, pl.ds(8 + cy, 8), columns_hit(8, 0))
            return carry

        lax.fori_loop(0, cx, row, 0)

    def lateral(r, i, low, high):
        old, new = fields[r], fields[r + 1]
        rows = pl.ds(PAD + low, high - low)
        beside = (old[i + 1, rows, :] + old[i + 3, rows, :]) + (
            old[i + 2, PAD - 1 + low:PAD - 1 + high, :] + old[i + 2, PAD + 1 + low:PAD + 1 + high, :])
        a = rate_b[i + 1, 8 + low:8 + high, :]
        b = coup_b[i + 1, 8 + low:8 + high, :]
        if r == 2:
            a, b = q3 * a, q3 * b
        a = jnp.concatenate([a] * reps, axis=1)
        b = jnp.concatenate([b] * reps, axis=1)
        out = a * old[i + 2, rows, :] - b * beside
        if r == 2:
            out = out + total[i + 1, 8 + low:8 + high, :]
        new[i + 2, rows, :] = out

    def inner(r, edge):
        def row(i, carry):
            lateral(r, i, 8, cy - 8)
            return carry

        lax.fori_loop(edge, cx - edge, row, 0)

    def rim(r):
        lateral(r, -1, 0, cy)
        lateral(r, cx, 0, cy)
        lateral(r, 0, -8, cy + 8)
        lateral(r, cx - 1, -8, cy + 8)

        def row(i, carry):
            lateral(r, i, -8, 8)
            lateral(r, i, cy - 8, cy + 8)
            return carry

        lax.fori_loop(1, cx - 1, row, 0)

    def rim_two(r):
        for i in (0, 1, cx - 2, cx - 1):
            lateral(r, i, 0, cy)

        def row(i, carry):
            lateral(r, i, 0, 8)
            lateral(r, i, cy - 8, cy)
            return carry

        lax.fori_loop(2, cx - 2, row, 0)

    def make_weights():
        pick = (iota((LANES, depth), 0) % depth == iota((LANES, depth), 1)).astype(F32)
        tiled = dot_t(dot_t(pick, vertical[...]), pick)
        same = iota((LANES, LANES), 0) // depth == iota((LANES, LANES), 1) // depth
        eye = jnp.where(iota((LANES, LANES), 0) == iota((LANES, LANES), 1), 1.0, 0.0)
        v1 = jnp.where(same, tiled, 0.0)
        v2 = dot(v1, v1)
        v3 = dot(v1, v2)
        polys = (
            q0 * eye + q1 * v1 + q2 * v2 + q3 * v3,
            q1 * eye + (2.0 * q2) * v1 + (3.0 * q3) * v2,
            q2 * eye + (3.0 * q3) * v1,
        )
        for k, poly in enumerate(polys):
            high, low = split2(poly)
            for row in (0, LANES):
                weights[k, row:row + LANES, 0:LANES] = high
                weights[k, row:row + LANES, LANES:2 * LANES] = low

    def depth_block(ks, i, count, low, high):
        cells = count * (high - low)
        for t in range(reps):
            lanes = slice(t * LANES, (t + 1) * LANES)
            out = None
            for k in ks:
                value = fields[k][pl.ds(i + 2, count), PAD + low:PAD + high, lanes].reshape(cells, LANES)
                both = jnp.concatenate(split2(value), axis=1)
                one = jnp.dot(both, weights[k], preferred_element_type=F32)
                out = one if out is None else out + one
            out = (out[:, 0:LANES] + out[:, LANES:2 * LANES]).reshape(count, high - low, LANES)
            spot = (pl.ds(i + 1, count), slice(8 + low, 8 + high), lanes)
            total[spot] = out if 0 in ks else total[spot] + out

    def depth_own(ks):
        def part(g, carry):
            depth_block(ks, g * GROUP, GROUP, 0, cy)
            return carry

        lax.fori_loop(0, cx // GROUP, part, 0)

    def depth_beside(ks):
        depth_block(ks, -1, 1, 0, cy)
        depth_block(ks, cx, 1, 0, cy)
        depth_block(ks, 0, cx, -8, 0)
        depth_block(ks, 0, cx, cy, cy + 8)

    hit = iota((sensors, sensors), 0) == jnp.broadcast_to(slots[...], (sensors, sensors))
    cell = jnp.sum(jnp.where(hit, jnp.broadcast_to(columns[...], (sensors, sensors)), 0), axis=1, keepdims=True)
    spots_v[...] = jnp.broadcast_to(cell, (sensors, LANES))
    to_scalars = pltpu.make_async_copy(spots_v, spots, spot_sem)
    to_scalars.start()

    spread_own()
    inner(0, 1)
    make_weights()
    depth_own((0,))
    for toward in range(4):
        @pl.when(coef_from(toward))
        def _():
            for part in range(2):
                coef_copy(toward, part).wait_recv()
    spread_beside()
    receive(0)
    rim(0)
    rim_two(1)
    send_corners(1)
    send_y(1)
    send_x(1)
    inner(1, 2)
    depth_own((1,))
    depth_own((2,))
    depth_beside((0, 1))
    inner(2, 1)
    receive(1)
    depth_beside((2,))
    rim(2)
    store = pltpu.make_async_copy(e3.at[pl.ds(2, cx), own, :], sample, store_sem)
    to_scalars.wait()

    parts = ready.shape[0] // sensors
    per = ready.shape[0] // n_gx
    mine = pl.ds(pl.multiple_of(me * per, per), per)

    def to_peer(i):
        peer = peer_of(i)
        return pltpu.make_async_remote_copy(
            src_ref=ready.at[pl.ds(pl.multiple_of(peer * per, per), per), :], dst_ref=grads.at[mine, :],
            send_sem=as_sem.at[i], recv_sem=ar_sem.at[i], device_id=(peer, my), device_id_type=MESH)

    def blocks_for(peer):
        for m in range(sensors // n_gx):
            k = peer * (sensors // n_gx) + m
            place = spots[k, 0]
            i = place // cy
            j = place % cy + PAD
            value = e3[i + 2, pl.ds(j, 1), :]
            mean = value[:, 0:LANES]
            for t in range(1, reps):
                mean = mean + value[:, t * LANES:(t + 1) * LANES]
            mean = (mean + pltpu.roll(mean, depth, axis=1)) * (depth / width)
            weight = (value - jnp.concatenate([mean] * reps, axis=1)) * 0.5
            along_x = weight * (e3[i + 3, pl.ds(j, 1), :] - e3[i + 1, pl.ds(j, 1), :])
            along_y = weight * (e3[i + 2, pl.ds(j + 1, 1), :] - e3[i + 2, pl.ds(j - 1, 1), :])
            for d, product in enumerate((along_x, along_y)):
                for t in range(reps):
                    ready[pl.ds(k * parts + d * reps + t, 1), :] = product[:, t * LANES:(t + 1) * LANES]

    batch = BATCH if n_gx % BATCH == 0 else 1

    def start(g, carry):
        turns = [1 + g * batch + b for b in range(batch)]
        for i in turns:
            blocks_for(peer_of(i))
        for i in turns:
            to_peer(i).start()
        return carry

    lax.fori_loop(0, n_gx // batch - 1, start, 0)
    for i in list(range(n_gx - batch + 1, n_gx)) + [0]:
        blocks_for(peer_of(i))
    for i in range(n_gx - batch + 1, n_gx):
        to_peer(i).start()
    keep = pltpu.make_async_copy(ready.at[mine, :], grads.at[mine, :], own_sem)
    keep.start()
    store.start()
    for r in range(2):
        sent(r)
    for toward in range(4):
        @pl.when(coef_has(toward))
        def _():
            for part in range(2):
                coef_copy(toward, part).wait_send()
    store.wait()
    keep.wait()

    def finish(i, carry):
        copy = to_peer(i)
        copy.wait_send()
        copy.wait_recv()
        return carry

    lax.fori_loop(1, n_gx, finish, 0)


def finish_kernel(sample_in, grads_in, sample, grads, rows, out_sem, store_sem):
    sensors, parts = rows.shape[0], rows.shape[1] // LANES
    cut = sample.shape[0] // 4
    spots = [pl.ds(p * cut, cut) for p in range(4)]
    stores = [pltpu.make_async_copy(sample_in.at[s], sample.at[s], store_sem.at[p]) for p, s in enumerate(spots)]
    for copy in stores:
        copy.start()
    for t in range(parts):
        rows[:, t * LANES:(t + 1) * LANES] = grads_in[pl.ds(t, sensors, stride=parts), :]
    last = pltpu.make_async_copy(rows, grads, out_sem)
    last.start()
    for store in stores:
        store.wait()
    last.wait()


def shards(n_gx, n_gy, noise, rate, coupling, vertical, coeffs, columns, slots):
    cx, cy, width = noise.shape
    sensors = slots.shape[1]
    parts = 2 * width // LANES
    hbm = pl.BlockSpec(memory_space=pltpu.HBM)
    vmem = pl.BlockSpec(memory_space=pltpu.VMEM)
    field = pltpu.VMEM((cx + 4, cy + 2 * PAD, width), F32)
    coef = pltpu.VMEM((cx + 2, cy + 16, LANES), F32)
    dma = pltpu.SemaphoreType.DMA
    sample, grads = pl.pallas_call(
        functools.partial(kernel, n_gx, n_gy),
        out_shape=(pltpu.VMEM(noise.shape, F32), pltpu.VMEM((sensors * parts, LANES), F32)),
        in_specs=[hbm] * 7,
        out_specs=(vmem, vmem),
        scratch_shapes=[
            pltpu.VMEM(rate.shape, F32), pltpu.VMEM(coupling.shape, F32), pltpu.VMEM(vertical.shape, F32),
            pltpu.VMEM(slots.shape, jnp.int32), pltpu.VMEM(columns.shape, jnp.int32), pltpu.SMEM(coeffs.shape, F32),
            field, field, field, field, pltpu.VMEM((cx + 2, cy + 16, width), F32),
            coef, coef,
            pltpu.VMEM((3, 2 * LANES, 2 * LANES), BF16),
            pltpu.VMEM((2, 2, 2 * cx, width), F32), pltpu.VMEM((2, 2, 2 * cx, width), F32),
            pltpu.VMEM((4, 2, cx, cy), F32),
            pltpu.VMEM((sensors, LANES), jnp.int32), pltpu.SMEM((sensors, LANES), jnp.int32),
            pltpu.VMEM((sensors * parts, LANES), F32),
            dma((6,)), dma((3,)), dma((2, 2)), dma((2, 2)), dma((2, 2)), dma((2, 2)),
            dma((2, 4)), dma((2, 4)), dma((4, 2)), dma((4, 2)),
            dma((n_gx,)), dma((n_gx,)), dma, dma, dma,
        ],
        compiler_params=pltpu.CompilerParams(
            collective_id=0, has_side_effects=True, vmem_limit_bytes=56 << 20),
    )(*(pltpu.with_memory_space_constraint(arg, pltpu.HBM)
        for arg in (noise, rate, coupling, vertical, slots, columns, coeffs)))
    return pl.pallas_call(
        finish_kernel,
        out_shape=(jax.ShapeDtypeStruct(noise.shape, F32),
                   jax.ShapeDtypeStruct((sensors, parts * LANES), F32)),
        in_specs=[pl.BlockSpec(memory_space=pltpu.VMEM)] * 2,
        out_specs=(hbm, hbm),
        scratch_shapes=[
            pltpu.VMEM((sensors, parts * LANES), F32), dma, dma((4,)),
        ],
        compiler_params=pltpu.CompilerParams(vmem_limit_bytes=16 << 20),
    )(sample, grads)


def solution(mesh):
    placed = (
        P("gx", "gy", None),
        P("gx", "gy"),
        P("gx", "gy"),
        P(),
        P(),
        P(("gx", "gy"), None),
        P(("gx", "gy"), None),
    )
    return jax.shard_map(
        functools.partial(shards, mesh.shape["gx"], mesh.shape["gy"]),
        mesh=mesh,
        in_specs=placed,
        out_specs=(P("gx", "gy", None), P(("gx", "gy"), None)),
        check_vma=False,
    )
```

```python
import functools

import jax
import jax.numpy as jnp
from jax import lax
from jax.experimental import pallas as pl
from jax.experimental.pallas import tpu as pltpu
from jax.sharding import PartitionSpec as P

MESH = pl.DeviceIdType.MESH
HIGHEST = lax.Precision.HIGHEST
F32 = jnp.float32
BF16 = jnp.bfloat16
LANES = 128
GROUP = 4
BATCH = 4
PAD = 16


def split2(value):
    high = value.astype(BF16)
    return high, (value - high.astype(F32)).astype(BF16)


def iota(shape, dim):
    return lax.broadcasted_iota(jnp.int32, shape, dim)


def dot_t(a, b):
    return lax.dot_general(a, b, (((1,), (1,)), ((), ())), precision=HIGHEST, preferred_element_type=F32)


def dot(a, b):
    return jnp.dot(a, b, precision=HIGHEST, preferred_element_type=F32)


def kernel(n_gx, n_gy, noise, rate_in, coupling_in, vertical_in, slots_in, columns_in, coeffs_in, sample, grads,
           rate, coupling, vertical, slots, columns, coeffs, e0, e1, e2, e3, total, rate_b, coup_b, weights,
           y_out, y_in, beside_coef, spots_v, spots, ready,
           small_sem, load_sem, xs_sem, xr_sem, ys_sem, yr_sem, cs_sem, cr_sem, ks_sem, kr_sem, as_sem, ar_sem, store_sem, own_sem, spot_sem):
    cx, cy, width = noise.shape
    depth = vertical.shape[0]
    sensors = slots.shape[1]
    reps = width // LANES
    me = lax.axis_index("gx")
    my = lax.axis_index("gy")
    fields = (e0, e1, e2, e3)
    own = pl.ds(PAD, cy)
    x_has = (me > 0, me < n_gx - 1)
    y_has = (my > 0, my < n_gy - 1)
    both_sides = [(sx, sy) for sx in range(2) for sy in range(2)]

    def x_at(side):
        return me - 1 if side == 0 else me + 1

    def y_at(side):
        return my - 1 if side == 0 else my + 1

    def peer_of(i):
        far = (i + 1) // 2
        return lax.rem(me + jnp.where(i % 2 == 1, far, n_gx - far), n_gx)

    barrier = pltpu.get_barrier_semaphore()

    beside_y = [(y_has[sy], (me, y_at(sy))) for sy in range(2)]
    beside_y += [(jnp.logical_and(x_has[sx], y_has[sy]), (x_at(sx), y_at(sy))) for sx, sy in both_sides]
    arrivals = n_gx - 1
    for there, device in beside_y:
        arrivals = arrivals + jnp.where(there, 1, 0)

        @pl.when(there)
        def _():
            pl.semaphore_signal(barrier, inc=1, device_id=device, device_id_type=MESH)

    def greet(s, carry):
        pl.semaphore_signal(barrier, inc=1, device_id=(peer_of(n_gx - 1 - s), my), device_id_type=MESH)
        return carry

    lax.fori_loop(0, n_gx - 1, greet, 0)
    loads = [
        pltpu.make_async_copy(noise.at[:, pl.ds(low, count), :], e0.at[pl.ds(2, cx), pl.ds(PAD + low, count), :], load_sem.at[i])
        for i, (low, count) in enumerate(((0, 8), (cy - 8, 8), (8, cy - 16)))
    ]
    for copy in loads:
        copy.start()
    small = [
        pltpu.make_async_copy(src, dst, small_sem.at[i])
        for i, (src, dst) in enumerate((
            (rate_in, rate), (coupling_in, coupling), (vertical_in, vertical),
            (slots_in, slots), (columns_in, columns), (coeffs_in, coeffs)))
    ]
    for copy in small:
        copy.start()

    for side in range(2):
        @pl.when(jnp.logical_not(x_has[side]))
        def _():
            for field in (e0, e2):
                for i in (0, 1) if side == 0 else (cx + 2, cx + 3):
                    field[i] = jnp.zeros(field.shape[1:], F32)
            beside_coef[1 - side] = jnp.zeros(beside_coef.shape[1:], F32)

        @pl.when(jnp.logical_not(y_has[side]))
        def _():
            for field in (e0, e2):
                for i in (1, cx + 2):
                    block = pl.ds(PAD - 8 if side == 0 else PAD + cy, 8)
                    field[i, block, :] = jnp.zeros((8, width), F32)
            for r in range(2):
                y_in[r, side] = jnp.zeros(y_in.shape[2:], F32)
            beside_coef[3 - side] = jnp.zeros(beside_coef.shape[1:], F32)

    pl.semaphore_wait(barrier, arrivals)

    def x_copy(r, side):
        field = fields[2 * r]
        row = 0 if side == 0 else cx - 2
        src = noise.at[pl.ds(row, 2)] if r == 0 else field.at[pl.ds(row + 2, 2), own, :]
        return pltpu.make_async_remote_copy(
            src_ref=src, dst_ref=field.at[pl.ds(cx + 2 if side == 0 else 0, 2), own, :],
            send_sem=xs_sem.at[r, side], recv_sem=xr_sem.at[r, side],
            device_id=(x_at(side), my), device_id_type=MESH)

    def y_copy(r, side):
        return pltpu.make_async_remote_copy(
            src_ref=y_out.at[r, side], dst_ref=y_in.at[r, 1 - side],
            send_sem=ys_sem.at[r, side], recv_sem=yr_sem.at[r, side],
            device_id=(me, y_at(side)), device_id_type=MESH)

    def corner_copy(r, sx, sy):
        field = fields[2 * r]
        row = 0 if sx == 0 else cx - 1
        col = 0 if sy == 0 else cy - 8
        src = noise.at[row, pl.ds(col, 8), :] if r == 0 else field.at[row + 2, pl.ds(PAD + col, 8), :]
        return pltpu.make_async_remote_copy(
            src_ref=src, dst_ref=field.at[cx + 2 if sx == 0 else 1, pl.ds(PAD + cy if sy == 0 else PAD - 8, 8), :],
            send_sem=cs_sem.at[r, 2 * sx + sy], recv_sem=cr_sem.at[r, 2 * sx + sy],
            device_id=(x_at(sx), y_at(sy)), device_id_type=MESH)

    def coef_copy(toward, part):
        return pltpu.make_async_remote_copy(
            src_ref=(rate_in, coupling_in)[part], dst_ref=beside_coef.at[toward, part],
            send_sem=ks_sem.at[toward, part], recv_sem=kr_sem.at[toward, part],
            device_id=(x_at(toward), my) if toward < 2 else (me, y_at(toward - 2)), device_id_type=MESH)

    def coef_has(toward):
        return x_has[toward] if toward < 2 else y_has[toward - 2]

    def coef_from(toward):
        return x_has[1 - toward] if toward < 2 else y_has[3 - toward]

    def send_corners(r):
        for sx, sy in both_sides:
            @pl.when(jnp.logical_and(x_has[sx], y_has[sy]))
            def _():
                corner_copy(r, sx, sy).start()

    def send_x(r):
        for side in range(2):
            @pl.when(x_has[side])
            def _():
                x_copy(r, side).start()

    def send_y(r):
        field = fields[2 * r]
        for i in range(cx):
            y_out[r, 0, 2 * i:2 * i + 2, :] = field[i + 2, PAD:PAD + 2, :]
            y_out[r, 1, 2 * i:2 * i + 2, :] = field[i + 2, PAD + cy - 2:PAD + cy, :]
        for side in range(2):
            @pl.when(y_has[side])
            def _():
                y_copy(r, side).start()

    def receive(r):
        field = fields[2 * r]
        for side in range(2):
            @pl.when(y_has[1 - side])
            def _():
                y_copy(r, side).wait_recv()
        for i in range(cx):
            field[i + 2, PAD - 2:PAD, :] = y_in[r, 0, 2 * i:2 * i + 2, :]
            field[i + 2, PAD + cy:PAD + cy + 2, :] = y_in[r, 1, 2 * i:2 * i + 2, :]
        for side in range(2):
            @pl.when(x_has[1 - side])
            def _():
                x_copy(r, side).wait_recv()
        for sx, sy in both_sides:
            @pl.when(jnp.logical_and(x_has[1 - sx], y_has[1 - sy]))
            def _():
                corner_copy(r, sx, sy).wait_recv()

    def sent(r):
        for side in range(2):
            @pl.when(x_has[side])
            def _():
                x_copy(r, side).wait_send()

            @pl.when(y_has[side])
            def _():
                y_copy(r, side).wait_send()
        for sx, sy in both_sides:
            @pl.when(jnp.logical_and(x_has[sx], y_has[sy]))
            def _():
                corner_copy(r, sx, sy).wait_send()

    send_corners(0)
    for toward in range(4):
        @pl.when(coef_has(toward))
        def _():
            for part in range(2):
                coef_copy(toward, part).start()
    loads[0].wait()
    loads[1].wait()
    send_y(0)
    send_x(0)
    for copy in small:
        copy.wait()
    loads[2].wait()

    q0 = coeffs[0] - coeffs[2]
    q1 = coeffs[1] - 3.0 * coeffs[3]
    q2 = 2.0 * coeffs[2]
    q3 = 4.0 * coeffs[3]

    def columns_hit(rows, first):
        return iota((rows, cy), 0) + first == iota((rows, cy), 1)

    def spread(src, dst, i, rows, hit):
        count = hit.shape[0]
        col = jnp.sum(jnp.where(hit, jnp.broadcast_to(src, (count, cy)), 0.0), axis=1, keepdims=True)
        dst[i, rows, :] = jnp.broadcast_to(col, (count, LANES))

    def spread_own():
        def row(i, carry):
            for src, dst in ((rate, rate_b), (coupling, coup_b)):
                spread(src[pl.ds(i, 1), :], dst, i + 1, pl.ds(8, cy), columns_hit(cy, 0))
            return carry

        lax.fori_loop(0, cx, row, 0)

    def spread_beside():
        for part, dst in enumerate((rate_b, coup_b)):
            spread(beside_coef[1, part, cx - 1:cx, :], dst, 0, pl.ds(8, cy), columns_hit(cy, 0))
            spread(beside_coef[0, part, 0:1, :], dst, cx + 1, pl.ds(8, cy), columns_hit(cy, 0))

        def row(i, carry):
            for part, dst in enumerate((rate_b, coup_b)):
                spread(beside_coef[3, part, pl.ds(i, 1), :], dst, i + 1, pl.ds(0, 8), columns_hit(8, cy - 8))
                spread(beside_coef[2, part, pl.ds(i, 1), :], dst, i + 1, pl.ds(8 + cy, 8), columns_hit(8, 0))
            return carry

        lax.fori_loop(0, cx, row, 0)

    def lateral(r, i, low, high):
        old, new = fields[r], fields[r + 1]
        rows = pl.ds(PAD + low, high - low)
        beside = (old[i + 1, rows, :] + old[i + 3, rows, :]) + (
            old[i + 2, PAD - 1 + low:PAD - 1 + high, :] + old[i + 2, PAD + 1 + low:PAD + 1 + high, :])
        a = rate_b[i + 1, 8 + low:8 + high, :]
        b = coup_b[i + 1, 8 + low:8 + high, :]
        if r == 2:
            a, b = q3 * a, q3 * b
        a = jnp.concatenate([a] * reps, axis=1)
        b = jnp.concatenate([b] * reps, axis=1)
        out = a * old[i + 2, rows, :] - b * beside
        if r == 2:
            out = out + total[i + 1, 8 + low:8 + high, :]
        new[i + 2, rows, :] = out

    def inner(r, edge):
        def row(i, carry):
            lateral(r, i, 8, cy - 8)
            return carry

        lax.fori_loop(edge, cx - edge, row, 0)

    def rim(r):
        lateral(r, -1, 0, cy)
        lateral(r, cx, 0, cy)
        lateral(r, 0, -8, cy + 8)
        lateral(r, cx - 1, -8, cy + 8)

        def row(i, carry):
            lateral(r, i, -8, 8)
            lateral(r, i, cy - 8, cy + 8)
            return carry

        lax.fori_loop(1, cx - 1, row, 0)

    def rim_rows(r):
        for i in (0, 1, cx - 2, cx - 1):
            lateral(r, i, 0, cy)

    def rim_columns(r):
        def row(i, carry):
            lateral(r, i, 0, 8)
            lateral(r, i, cy - 8, cy)
            return carry

        lax.fori_loop(2, cx - 2, row, 0)

    def make_weights():
        pick = (iota((LANES, depth), 0) % depth == iota((LANES, depth), 1)).astype(F32)
        tiled = dot_t(dot_t(pick, vertical[...]), pick)
        same = iota((LANES, LANES), 0) // depth == iota((LANES, LANES), 1) // depth
        eye = jnp.where(iota((LANES, LANES), 0) == iota((LANES, LANES), 1), 1.0, 0.0)
        v1 = jnp.where(same, tiled, 0.0)
        v2 = dot(v1, v1)
        v3 = dot(v1, v2)
        polys = (
            q0 * eye + q1 * v1 + q2 * v2 + q3 * v3,
            q1 * eye + (2.0 * q2) * v1 + (3.0 * q3) * v2,
            q2 * eye + (3.0 * q3) * v1,
        )
        for k, poly in enumerate(polys):
            high, low = split2(poly)
            for row in (0, LANES):
                weights[k, row:row + LANES, 0:LANES] = high
                weights[k, row:row + LANES, LANES:2 * LANES] = low

    def depth_block(ks, i, count, low, high):
        cells = count * (high - low)
        for t in range(reps):
            lanes = slice(t * LANES, (t + 1) * LANES)
            out = None
            for k in ks:
                value = fields[k][pl.ds(i + 2, count), PAD + low:PAD + high, lanes].reshape(cells, LANES)
                both = jnp.concatenate(split2(value), axis=1)
                one = jnp.dot(both, weights[k], preferred_element_type=F32)
                out = one if out is None else out + one
            out = (out[:, 0:LANES] + out[:, LANES:2 * LANES]).reshape(count, high - low, LANES)
            spot = (pl.ds(i + 1, count), slice(8 + low, 8 + high), lanes)
            total[spot] = out if 0 in ks else total[spot] + out

    def depth_own(ks):
        def part(g, carry):
            depth_block(ks, g * GROUP, GROUP, 0, cy)
            return carry

        lax.fori_loop(0, cx // GROUP, part, 0)

    def depth_beside(ks):
        depth_block(ks, -1, 1, 0, cy)
        depth_block(ks, cx, 1, 0, cy)
        depth_block(ks, 0, cx, -8, 0)
        depth_block(ks, 0, cx, cy, cy + 8)

    hit = iota((sensors, sensors), 0) == jnp.broadcast_to(slots[...], (sensors, sensors))
    cell = jnp.sum(jnp.where(hit, jnp.broadcast_to(columns[...], (sensors, sensors)), 0), axis=1, keepdims=True)
    spots_v[...] = jnp.broadcast_to(cell, (sensors, LANES))
    to_scalars = pltpu.make_async_copy(spots_v, spots, spot_sem)
    to_scalars.start()

    spread_own()
    inner(0, 1)
    make_weights()
    depth_own((0,))
    for toward in range(4):
        @pl.when(coef_from(toward))
        def _():
            for part in range(2):
                coef_copy(toward, part).wait_recv()
    spread_beside()
    receive(0)
    rim(0)
    rim_rows(1)
    send_corners(1)
    send_x(1)
    rim_columns(1)
    send_y(1)
    inner(1, 2)
    depth_own((1,))
    depth_own((2,))
    depth_beside((0, 1))
    inner(2, 1)
    receive(1)
    depth_beside((2,))
    rim(2)
    store = pltpu.make_async_copy(e3.at[pl.ds(2, cx), own, :], sample, store_sem)
    to_scalars.wait()

    parts = ready.shape[0] // sensors
    per = ready.shape[0] // n_gx
    mine = pl.ds(pl.multiple_of(me * per, per), per)

    def to_peer(i):
        peer = peer_of(i)
        return pltpu.make_async_remote_copy(
            src_ref=ready.at[pl.ds(pl.multiple_of(peer * per, per), per), :], dst_ref=grads.at[mine, :],
            send_sem=as_sem.at[i], recv_sem=ar_sem.at[i], device_id=(peer, my), device_id_type=MESH)

    def blocks_for(peer):
        for m in range(sensors // n_gx):
            k = peer * (sensors // n_gx) + m
            place = spots[k, 0]
            i = place // cy
            j = place % cy + PAD
            value = e3[i + 2, pl.ds(j, 1), :]
            mean = value[:, 0:LANES]
            for t in range(1, reps):
                mean = mean + value[:, t * LANES:(t + 1) * LANES]
            mean = (mean + pltpu.roll(mean, depth, axis=1)) * (depth / width)
            weight = (value - jnp.concatenate([mean] * reps, axis=1)) * 0.5
            along_x = weight * (e3[i + 3, pl.ds(j, 1), :] - e3[i + 1, pl.ds(j, 1), :])
            along_y = weight * (e3[i + 2, pl.ds(j + 1, 1), :] - e3[i + 2, pl.ds(j - 1, 1), :])
            for d, product in enumerate((along_x, along_y)):
                for t in range(reps):
                    ready[pl.ds(k * parts + d * reps + t, 1), :] = product[:, t * LANES:(t + 1) * LANES]

    batch = BATCH if n_gx % BATCH == 0 else 1

    def start(g, carry):
        turns = [1 + g * batch + b for b in range(batch)]
        for i in turns:
            blocks_for(peer_of(i))
        for i in turns:
            to_peer(i).start()
        return carry

    lax.fori_loop(0, n_gx // batch - 1, start, 0)
    for i in list(range(n_gx - batch + 1, n_gx)) + [0]:
        blocks_for(peer_of(i))
    for i in range(n_gx - batch + 1, n_gx):
        to_peer(i).start()
    keep = pltpu.make_async_copy(ready.at[mine, :], grads.at[mine, :], own_sem)
    keep.start()
    store.start()
    for r in range(2):
        sent(r)
    for toward in range(4):
        @pl.when(coef_has(toward))
        def _():
            for part in range(2):
                coef_copy(toward, part).wait_send()
    store.wait()
    keep.wait()

    def finish(i, carry):
        copy = to_peer(i)
        copy.wait_send()
        copy.wait_recv()
        return carry

    lax.fori_loop(1, n_gx, finish, 0)


def finish_kernel(sample_in, grads_in, sample, grads, rows, out_sem, store_sem):
    sensors, parts = rows.shape[0], rows.shape[1] // LANES
    cut = sample.shape[0] // 4
    spots = [pl.ds(p * cut, cut) for p in range(4)]
    stores = [pltpu.make_async_copy(sample_in.at[s], sample.at[s], store_sem.at[p]) for p, s in enumerate(spots)]
    for copy in stores:
        copy.start()
    for t in range(parts):
        rows[:, t * LANES:(t + 1) * LANES] = grads_in[pl.ds(t, sensors, stride=parts), :]
    last = pltpu.make_async_copy(rows, grads, out_sem)
    last.start()
    for store in stores:
        store.wait()
    last.wait()


def shards(n_gx, n_gy, noise, rate, coupling, vertical, coeffs, columns, slots):
    cx, cy, width = noise.shape
    sensors = slots.shape[1]
    parts = 2 * width // LANES
    hbm = pl.BlockSpec(memory_space=pltpu.HBM)
    vmem = pl.BlockSpec(memory_space=pltpu.VMEM)
    field = pltpu.VMEM((cx + 4, cy + 2 * PAD, width), F32)
    coef = pltpu.VMEM((cx + 2, cy + 16, LANES), F32)
    dma = pltpu.SemaphoreType.DMA
    sample, grads = pl.pallas_call(
        functools.partial(kernel, n_gx, n_gy),
        out_shape=(pltpu.VMEM(noise.shape, F32), pltpu.VMEM((sensors * parts, LANES), F32)),
        in_specs=[hbm] * 7,
        out_specs=(vmem, vmem),
        scratch_shapes=[
            pltpu.VMEM(rate.shape, F32), pltpu.VMEM(coupling.shape, F32), pltpu.VMEM(vertical.shape, F32),
            pltpu.VMEM(slots.shape, jnp.int32), pltpu.VMEM(columns.shape, jnp.int32), pltpu.SMEM(coeffs.shape, F32),
            field, field, field, field, pltpu.VMEM((cx + 2, cy + 16, width), F32),
            coef, coef,
            pltpu.VMEM((3, 2 * LANES, 2 * LANES), BF16),
            pltpu.VMEM((2, 2, 2 * cx, width), F32), pltpu.VMEM((2, 2, 2 * cx, width), F32),
            pltpu.VMEM((4, 2, cx, cy), F32),
            pltpu.VMEM((sensors, LANES), jnp.int32), pltpu.SMEM((sensors, LANES), jnp.int32),
            pltpu.VMEM((sensors * parts, LANES), F32),
            dma((6,)), dma((3,)), dma((2, 2)), dma((2, 2)), dma((2, 2)), dma((2, 2)),
            dma((2, 4)), dma((2, 4)), dma((4, 2)), dma((4, 2)),
            dma((n_gx,)), dma((n_gx,)), dma, dma, dma,
        ],
        compiler_params=pltpu.CompilerParams(
            collective_id=0, has_side_effects=True, vmem_limit_bytes=56 << 20),
    )(*(pltpu.with_memory_space_constraint(arg, pltpu.HBM)
        for arg in (noise, rate, coupling, vertical, slots, columns, coeffs)))
    return pl.pallas_call(
        finish_kernel,
        out_shape=(jax.ShapeDtypeStruct(noise.shape, F32),
                   jax.ShapeDtypeStruct((sensors, parts * LANES), F32)),
        in_specs=[pl.BlockSpec(memory_space=pltpu.VMEM)] * 2,
        out_specs=(hbm, hbm),
        scratch_shapes=[
            pltpu.VMEM((sensors, parts * LANES), F32), dma, dma((4,)),
        ],
        compiler_params=pltpu.CompilerParams(vmem_limit_bytes=16 << 20),
    )(sample, grads)


def solution(mesh):
    placed = (
        P("gx", "gy", None),
        P("gx", "gy"),
        P("gx", "gy"),
        P(),
        P(),
        P(("gx", "gy"), None),
        P(("gx", "gy"), None),
    )
    return jax.shard_map(
        functools.partial(shards, mesh.shape["gx"], mesh.shape["gy"]),
        mesh=mesh,
        in_specs=placed,
        out_specs=(P("gx", "gy", None), P(("gx", "gy"), None)),
        check_vma=False,
    )
```

```python
import functools

import jax
import jax.numpy as jnp
from jax import lax
from jax.experimental import pallas as pl
from jax.experimental.pallas import tpu as pltpu
from jax.sharding import PartitionSpec as P

MESH = pl.DeviceIdType.MESH
HIGHEST = lax.Precision.HIGHEST
F32 = jnp.float32
BF16 = jnp.bfloat16
LANES = 128
GROUP = 4
BATCH = 4
PAD = 16


def split2(value):
    high = value.astype(BF16)
    return high, (value - high.astype(F32)).astype(BF16)


def iota(shape, dim):
    return lax.broadcasted_iota(jnp.int32, shape, dim)


def dot_t(a, b):
    return lax.dot_general(a, b, (((1,), (1,)), ((), ())), precision=HIGHEST, preferred_element_type=F32)


def dot(a, b):
    return jnp.dot(a, b, precision=HIGHEST, preferred_element_type=F32)


def kernel(n_gx, n_gy, noise, rate_in, coupling_in, vertical_in, slots_in, columns_in, coeffs_in, sample, grads,
           rate, coupling, vertical, slots, columns, coeffs, e0, e1, e2, e3, total, rate_b, coup_b, weights,
           y_out, y_in, beside_coef, spots_v, spots, ready,
           small_sem, load_sem, xs_sem, xr_sem, ys_sem, yr_sem, cs_sem, cr_sem, ks_sem, kr_sem, as_sem, ar_sem, store_sem, own_sem, spot_sem):
    cx, cy, width = noise.shape
    depth = vertical.shape[0]
    sensors = slots.shape[1]
    reps = width // LANES
    me = lax.axis_index("gx")
    my = lax.axis_index("gy")
    fields = (e0, e1, e2, e3)
    own = pl.ds(PAD, cy)
    x_has = (me > 0, me < n_gx - 1)
    y_has = (my > 0, my < n_gy - 1)
    both_sides = [(sx, sy) for sx in range(2) for sy in range(2)]

    def x_at(side):
        return me - 1 if side == 0 else me + 1

    def y_at(side):
        return my - 1 if side == 0 else my + 1

    def peer_of(i):
        far = (i + 1) // 2
        return lax.rem(me + jnp.where(i % 2 == 1, far, n_gx - far), n_gx)

    barrier = pltpu.get_barrier_semaphore()

    beside_y = [(y_has[sy], (me, y_at(sy))) for sy in range(2)]
    beside_y += [(jnp.logical_and(x_has[sx], y_has[sy]), (x_at(sx), y_at(sy))) for sx, sy in both_sides]
    arrivals = n_gx - 1
    for there, device in beside_y:
        arrivals = arrivals + jnp.where(there, 1, 0)

        @pl.when(there)
        def _():
            pl.semaphore_signal(barrier, inc=1, device_id=device, device_id_type=MESH)

    def greet(s, carry):
        pl.semaphore_signal(barrier, inc=1, device_id=(peer_of(n_gx - 1 - s), my), device_id_type=MESH)
        return carry

    lax.fori_loop(0, n_gx - 1, greet, 0)
    loads = [
        pltpu.make_async_copy(noise.at[:, pl.ds(low, count), :], e0.at[pl.ds(2, cx), pl.ds(PAD + low, count), :], load_sem.at[i])
        for i, (low, count) in enumerate(((0, 8), (cy - 8, 8), (8, cy - 16)))
    ]
    for copy in loads:
        copy.start()
    small = [
        pltpu.make_async_copy(src, dst, small_sem.at[i])
        for i, (src, dst) in enumerate((
            (rate_in, rate), (coupling_in, coupling), (vertical_in, vertical),
            (slots_in, slots), (columns_in, columns), (coeffs_in, coeffs)))
    ]
    for copy in small:
        copy.start()

    for side in range(2):
        @pl.when(jnp.logical_not(x_has[side]))
        def _():
            for field in (e0, e2):
                for i in (0, 1) if side == 0 else (cx + 2, cx + 3):
                    field[i] = jnp.zeros(field.shape[1:], F32)
            beside_coef[1 - side] = jnp.zeros(beside_coef.shape[1:], F32)

        @pl.when(jnp.logical_not(y_has[side]))
        def _():
            for field in (e0, e2):
                for i in (1, cx + 2):
                    block = pl.ds(PAD - 8 if side == 0 else PAD + cy, 8)
                    field[i, block, :] = jnp.zeros((8, width), F32)
            for r in range(2):
                y_in[r, side] = jnp.zeros(y_in.shape[2:], F32)
            beside_coef[3 - side] = jnp.zeros(beside_coef.shape[1:], F32)

    pl.semaphore_wait(barrier, arrivals)

    def x_copy(r, side):
        field = fields[2 * r]
        row = 0 if side == 0 else cx - 2
        src = noise.at[pl.ds(row, 2)] if r == 0 else field.at[pl.ds(row + 2, 2), own, :]
        return pltpu.make_async_remote_copy(
            src_ref=src, dst_ref=field.at[pl.ds(cx + 2 if side == 0 else 0, 2), own, :],
            send_sem=xs_sem.at[r, side], recv_sem=xr_sem.at[r, side],
            device_id=(x_at(side), my), device_id_type=MESH)

    def y_copy(r, side):
        return pltpu.make_async_remote_copy(
            src_ref=y_out.at[r, side], dst_ref=y_in.at[r, 1 - side],
            send_sem=ys_sem.at[r, side], recv_sem=yr_sem.at[r, side],
            device_id=(me, y_at(side)), device_id_type=MESH)

    def corner_copy(r, sx, sy):
        field = fields[2 * r]
        row = 0 if sx == 0 else cx - 1
        col = 0 if sy == 0 else cy - 8
        src = noise.at[row, pl.ds(col, 8), :] if r == 0 else field.at[row + 2, pl.ds(PAD + col, 8), :]
        return pltpu.make_async_remote_copy(
            src_ref=src, dst_ref=field.at[cx + 2 if sx == 0 else 1, pl.ds(PAD + cy if sy == 0 else PAD - 8, 8), :],
            send_sem=cs_sem.at[r, 2 * sx + sy], recv_sem=cr_sem.at[r, 2 * sx + sy],
            device_id=(x_at(sx), y_at(sy)), device_id_type=MESH)

    def coef_copy(toward, part):
        return pltpu.make_async_remote_copy(
            src_ref=(rate_in, coupling_in)[part], dst_ref=beside_coef.at[toward, part],
            send_sem=ks_sem.at[toward, part], recv_sem=kr_sem.at[toward, part],
            device_id=(x_at(toward), my) if toward < 2 else (me, y_at(toward - 2)), device_id_type=MESH)

    def coef_has(toward):
        return x_has[toward] if toward < 2 else y_has[toward - 2]

    def coef_from(toward):
        return x_has[1 - toward] if toward < 2 else y_has[3 - toward]

    def send_corners(r):
        for sx, sy in both_sides:
            @pl.when(jnp.logical_and(x_has[sx], y_has[sy]))
            def _():
                corner_copy(r, sx, sy).start()

    def send_x(r):
        for side in range(2):
            @pl.when(x_has[side])
            def _():
                x_copy(r, side).start()

    def send_y(r):
        field = fields[2 * r]
        for i in range(cx):
            y_out[r, 0, 2 * i:2 * i + 2, :] = field[i + 2, PAD:PAD + 2, :]
            y_out[r, 1, 2 * i:2 * i + 2, :] = field[i + 2, PAD + cy - 2:PAD + cy, :]
        for side in range(2):
            @pl.when(y_has[side])
            def _():
                y_copy(r, side).start()

    def receive_y(r):
        field = fields[2 * r]
        for side in range(2):
            @pl.when(y_has[1 - side])
            def _():
                y_copy(r, side).wait_recv()
        for i in range(cx):
            field[i + 2, PAD - 2:PAD, :] = y_in[r, 0, 2 * i:2 * i + 2, :]
            field[i + 2, PAD + cy:PAD + cy + 2, :] = y_in[r, 1, 2 * i:2 * i + 2, :]

    def receive_x(r):
        for side in range(2):
            @pl.when(x_has[1 - side])
            def _():
                x_copy(r, side).wait_recv()
        for sx, sy in both_sides:
            @pl.when(jnp.logical_and(x_has[1 - sx], y_has[1 - sy]))
            def _():
                corner_copy(r, sx, sy).wait_recv()

    def sent(r):
        for side in range(2):
            @pl.when(x_has[side])
            def _():
                x_copy(r, side).wait_send()

            @pl.when(y_has[side])
            def _():
                y_copy(r, side).wait_send()
        for sx, sy in both_sides:
            @pl.when(jnp.logical_and(x_has[sx], y_has[sy]))
            def _():
                corner_copy(r, sx, sy).wait_send()

    send_corners(0)
    for toward in range(4):
        @pl.when(coef_has(toward))
        def _():
            for part in range(2):
                coef_copy(toward, part).start()
    loads[0].wait()
    loads[1].wait()
    send_y(0)
    send_x(0)
    for copy in small:
        copy.wait()
    loads[2].wait()

    q0 = coeffs[0] - coeffs[2]
    q1 = coeffs[1] - 3.0 * coeffs[3]
    q2 = 2.0 * coeffs[2]
    q3 = 4.0 * coeffs[3]

    def columns_hit(rows, first):
        return iota((rows, cy), 0) + first == iota((rows, cy), 1)

    def spread(src, dst, i, rows, hit):
        count = hit.shape[0]
        col = jnp.sum(jnp.where(hit, jnp.broadcast_to(src, (count, cy)), 0.0), axis=1, keepdims=True)
        dst[i, rows, :] = jnp.broadcast_to(col, (count, LANES))

    def spread_own():
        def row(i, carry):
            for src, dst in ((rate, rate_b), (coupling, coup_b)):
                spread(src[pl.ds(i, 1), :], dst, i + 1, pl.ds(8, cy), columns_hit(cy, 0))
            return carry

        lax.fori_loop(0, cx, row, 0)

    def spread_beside():
        for part, dst in enumerate((rate_b, coup_b)):
            spread(beside_coef[1, part, cx - 1:cx, :], dst, 0, pl.ds(8, cy), columns_hit(cy, 0))
            spread(beside_coef[0, part, 0:1, :], dst, cx + 1, pl.ds(8, cy), columns_hit(cy, 0))

        def row(i, carry):
            for part, dst in enumerate((rate_b, coup_b)):
                spread(beside_coef[3, part, pl.ds(i, 1), :], dst, i + 1, pl.ds(0, 8), columns_hit(8, cy - 8))
                spread(beside_coef[2, part, pl.ds(i, 1), :], dst, i + 1, pl.ds(8 + cy, 8), columns_hit(8, 0))
            return carry

        lax.fori_loop(0, cx, row, 0)

    def lateral(r, i, low, high):
        old, new = fields[r], fields[r + 1]
        rows = pl.ds(PAD + low, high - low)
        beside = (old[i + 1, rows, :] + old[i + 3, rows, :]) + (
            old[i + 2, PAD - 1 + low:PAD - 1 + high, :] + old[i + 2, PAD + 1 + low:PAD + 1 + high, :])
        a = rate_b[i + 1, 8 + low:8 + high, :]
        b = coup_b[i + 1, 8 + low:8 + high, :]
        if r == 2:
            a, b = q3 * a, q3 * b
        a = jnp.concatenate([a] * reps, axis=1)
        b = jnp.concatenate([b] * reps, axis=1)
        out = a * old[i + 2, rows, :] - b * beside
        if r == 2:
            out = out + total[i + 1, 8 + low:8 + high, :]
        new[i + 2, rows, :] = out

    def inner(r, edge):
        def row(i, carry):
            lateral(r, i, 8, cy - 8)
            return carry

        lax.fori_loop(edge, cx - edge, row, 0)

    def rim_y(r):
        def row(i, carry):
            lateral(r, i, -8, 8)
            lateral(r, i, cy - 8, cy + 8)
            return carry

        lax.fori_loop(1, cx - 1, row, 0)

    def rim_x(r):
        lateral(r, -1, 0, cy)
        lateral(r, cx, 0, cy)
        lateral(r, 0, -8, cy + 8)
        lateral(r, cx - 1, -8, cy + 8)

    def rim_rows(r):
        for i in (0, 1, cx - 2, cx - 1):
            lateral(r, i, 0, cy)

    def rim_columns(r):
        def row(i, carry):
            lateral(r, i, 0, 8)
            lateral(r, i, cy - 8, cy)
            return carry

        lax.fori_loop(2, cx - 2, row, 0)

    def make_weights():
        pick = (iota((LANES, depth), 0) % depth == iota((LANES, depth), 1)).astype(F32)
        tiled = dot_t(dot_t(pick, vertical[...]), pick)
        same = iota((LANES, LANES), 0) // depth == iota((LANES, LANES), 1) // depth
        eye = jnp.where(iota((LANES, LANES), 0) == iota((LANES, LANES), 1), 1.0, 0.0)
        v1 = jnp.where(same, tiled, 0.0)
        v2 = dot(v1, v1)
        v3 = dot(v1, v2)
        polys = (
            q0 * eye + q1 * v1 + q2 * v2 + q3 * v3,
            q1 * eye + (2.0 * q2) * v1 + (3.0 * q3) * v2,
            q2 * eye + (3.0 * q3) * v1,
        )
        for k, poly in enumerate(polys):
            high, low = split2(poly)
            for row in (0, LANES):
                weights[k, row:row + LANES, 0:LANES] = high
                weights[k, row:row + LANES, LANES:2 * LANES] = low

    def depth_block(ks, i, count, low, high):
        cells = count * (high - low)
        for t in range(reps):
            lanes = slice(t * LANES, (t + 1) * LANES)
            out = None
            for k in ks:
                value = fields[k][pl.ds(i + 2, count), PAD + low:PAD + high, lanes].reshape(cells, LANES)
                both = jnp.concatenate(split2(value), axis=1)
                one = jnp.dot(both, weights[k], preferred_element_type=F32)
                out = one if out is None else out + one
            out = (out[:, 0:LANES] + out[:, LANES:2 * LANES]).reshape(count, high - low, LANES)
            spot = (pl.ds(i + 1, count), slice(8 + low, 8 + high), lanes)
            total[spot] = out if 0 in ks else total[spot] + out

    def depth_own(ks):
        def part(g, carry):
            depth_block(ks, g * GROUP, GROUP, 0, cy)
            return carry

        lax.fori_loop(0, cx // GROUP, part, 0)

    def depth_x(ks):
        depth_block(ks, -1, 1, 0, cy)
        depth_block(ks, cx, 1, 0, cy)

    def depth_y(ks):
        depth_block(ks, 0, cx, -8, 0)
        depth_block(ks, 0, cx, cy, cy + 8)

    hit = iota((sensors, sensors), 0) == jnp.broadcast_to(slots[...], (sensors, sensors))
    cell = jnp.sum(jnp.where(hit, jnp.broadcast_to(columns[...], (sensors, sensors)), 0), axis=1, keepdims=True)
    spots_v[...] = jnp.broadcast_to(cell, (sensors, LANES))
    to_scalars = pltpu.make_async_copy(spots_v, spots, spot_sem)
    to_scalars.start()

    spread_own()
    inner(0, 1)
    make_weights()
    depth_own((0,))
    for toward in range(4):
        @pl.when(coef_from(toward))
        def _():
            for part in range(2):
                coef_copy(toward, part).wait_recv()
    spread_beside()
    receive_y(0)
    rim_y(0)
    receive_x(0)
    rim_x(0)
    rim_rows(1)
    send_corners(1)
    send_x(1)
    rim_columns(1)
    send_y(1)
    inner(1, 2)
    depth_own((1,))
    depth_own((2,))
    depth_x((0, 1))
    depth_y((0, 1))
    inner(2, 1)
    receive_y(1)
    depth_y((2,))
    rim_y(2)
    receive_x(1)
    depth_x((2,))
    rim_x(2)
    store = pltpu.make_async_copy(e3.at[pl.ds(2, cx), own, :], sample, store_sem)
    to_scalars.wait()

    parts = ready.shape[0] // sensors
    per = ready.shape[0] // n_gx
    mine = pl.ds(pl.multiple_of(me * per, per), per)

    def to_peer(i):
        peer = peer_of(i)
        return pltpu.make_async_remote_copy(
            src_ref=ready.at[pl.ds(pl.multiple_of(peer * per, per), per), :], dst_ref=grads.at[mine, :],
            send_sem=as_sem.at[i], recv_sem=ar_sem.at[i], device_id=(peer, my), device_id_type=MESH)

    def blocks_for(peer):
        for m in range(sensors // n_gx):
            k = peer * (sensors // n_gx) + m
            place = spots[k, 0]
            i = place // cy
            j = place % cy + PAD
            value = e3[i + 2, pl.ds(j, 1), :]
            mean = value[:, 0:LANES]
            for t in range(1, reps):
                mean = mean + value[:, t * LANES:(t + 1) * LANES]
            mean = (mean + pltpu.roll(mean, depth, axis=1)) * (depth / width)
            weight = (value - jnp.concatenate([mean] * reps, axis=1)) * 0.5
            along_x = weight * (e3[i + 3, pl.ds(j, 1), :] - e3[i + 1, pl.ds(j, 1), :])
            along_y = weight * (e3[i + 2, pl.ds(j + 1, 1), :] - e3[i + 2, pl.ds(j - 1, 1), :])
            for d, product in enumerate((along_x, along_y)):
                for t in range(reps):
                    ready[pl.ds(k * parts + d * reps + t, 1), :] = product[:, t * LANES:(t + 1) * LANES]

    batch = BATCH if n_gx % BATCH == 0 else 1

    def start(g, carry):
        turns = [1 + g * batch + b for b in range(batch)]
        for i in turns:
            blocks_for(peer_of(i))
        for i in turns:
            to_peer(i).start()
        return carry

    lax.fori_loop(0, n_gx // batch - 1, start, 0)
    for i in list(range(n_gx - batch + 1, n_gx)) + [0]:
        blocks_for(peer_of(i))
    for i in range(n_gx - batch + 1, n_gx):
        to_peer(i).start()
    keep = pltpu.make_async_copy(ready.at[mine, :], grads.at[mine, :], own_sem)
    keep.start()
    store.start()
    for r in range(2):
        sent(r)
    for toward in range(4):
        @pl.when(coef_has(toward))
        def _():
            for part in range(2):
                coef_copy(toward, part).wait_send()
    store.wait()
    keep.wait()

    def finish(i, carry):
        copy = to_peer(i)
        copy.wait_send()
        copy.wait_recv()
        return carry

    lax.fori_loop(1, n_gx, finish, 0)


def finish_kernel(sample_in, grads_in, sample, grads, rows, out_sem, store_sem):
    sensors, parts = rows.shape[0], rows.shape[1] // LANES
    cut = sample.shape[0] // 4
    spots = [pl.ds(p * cut, cut) for p in range(4)]
    stores = [pltpu.make_async_copy(sample_in.at[s], sample.at[s], store_sem.at[p]) for p, s in enumerate(spots)]
    for copy in stores:
        copy.start()
    for t in range(parts):
        rows[:, t * LANES:(t + 1) * LANES] = grads_in[pl.ds(t, sensors, stride=parts), :]
    last = pltpu.make_async_copy(rows, grads, out_sem)
    last.start()
    for store in stores:
        store.wait()
    last.wait()


def shards(n_gx, n_gy, noise, rate, coupling, vertical, coeffs, columns, slots):
    cx, cy, width = noise.shape
    sensors = slots.shape[1]
    parts = 2 * width // LANES
    hbm = pl.BlockSpec(memory_space=pltpu.HBM)
    vmem = pl.BlockSpec(memory_space=pltpu.VMEM)
    field = pltpu.VMEM((cx + 4, cy + 2 * PAD, width), F32)
    coef = pltpu.VMEM((cx + 2, cy + 16, LANES), F32)
    dma = pltpu.SemaphoreType.DMA
    sample, grads = pl.pallas_call(
        functools.partial(kernel, n_gx, n_gy),
        out_shape=(pltpu.VMEM(noise.shape, F32), pltpu.VMEM((sensors * parts, LANES), F32)),
        in_specs=[hbm] * 7,
        out_specs=(vmem, vmem),
        scratch_shapes=[
            pltpu.VMEM(rate.shape, F32), pltpu.VMEM(coupling.shape, F32), pltpu.VMEM(vertical.shape, F32),
            pltpu.VMEM(slots.shape, jnp.int32), pltpu.VMEM(columns.shape, jnp.int32), pltpu.SMEM(coeffs.shape, F32),
            field, field, field, field, pltpu.VMEM((cx + 2, cy + 16, width), F32),
            coef, coef,
            pltpu.VMEM((3, 2 * LANES, 2 * LANES), BF16),
            pltpu.VMEM((2, 2, 2 * cx, width), F32), pltpu.VMEM((2, 2, 2 * cx, width), F32),
            pltpu.VMEM((4, 2, cx, cy), F32),
            pltpu.VMEM((sensors, LANES), jnp.int32), pltpu.SMEM((sensors, LANES), jnp.int32),
            pltpu.VMEM((sensors * parts, LANES), F32),
            dma((6,)), dma((3,)), dma((2, 2)), dma((2, 2)), dma((2, 2)), dma((2, 2)),
            dma((2, 4)), dma((2, 4)), dma((4, 2)), dma((4, 2)),
            dma((n_gx,)), dma((n_gx,)), dma, dma, dma,
        ],
        compiler_params=pltpu.CompilerParams(
            collective_id=0, has_side_effects=True, vmem_limit_bytes=56 << 20),
    )(*(pltpu.with_memory_space_constraint(arg, pltpu.HBM)
        for arg in (noise, rate, coupling, vertical, slots, columns, coeffs)))
    return pl.pallas_call(
        finish_kernel,
        out_shape=(jax.ShapeDtypeStruct(noise.shape, F32),
                   jax.ShapeDtypeStruct((sensors, parts * LANES), F32)),
        in_specs=[pl.BlockSpec(memory_space=pltpu.VMEM)] * 2,
        out_specs=(hbm, hbm),
        scratch_shapes=[
            pltpu.VMEM((sensors, parts * LANES), F32), dma, dma((4,)),
        ],
        compiler_params=pltpu.CompilerParams(vmem_limit_bytes=16 << 20),
    )(sample, grads)


def solution(mesh):
    placed = (
        P("gx", "gy", None),
        P("gx", "gy"),
        P("gx", "gy"),
        P(),
        P(),
        P(("gx", "gy"), None),
        P(("gx", "gy"), None),
    )
    return jax.shard_map(
        functools.partial(shards, mesh.shape["gx"], mesh.shape["gy"]),
        mesh=mesh,
        in_specs=placed,
        out_specs=(P("gx", "gy", None), P(("gx", "gy"), None)),
        check_vma=False,
    )
```
